128 devices in a mesh: mem: 4 (over x), lat: 32 (over z, y, core).
Axes of the slice: x: 4, y: 4, z: 4, core: 2. Of those that a mesh axis runs over, the one named last changes fastest.
Arguments:
- prior_member_stack: float32 [64, 16, 256, 512], P('mem', None, 'lat'), may hold values from -6 to 6
- zonal_stability_ratio: float32 [256, 512], P('lat'), may hold values from -0.45 to 0.45
- meridional_stability_ratio: float32 [256, 512], P('lat'), may hold values from -0.45 to 0.45
- obs_perturb: bfloat16 [2048, 64, 4096], P(('mem', 'lat')), may hold values from -2 to 2
- innovation: float32 [2048, 4096], P(('mem', 'lat')), may hold values from -6 to 6
- inverse_error_variance: float32 [2048, 4096], P(('mem', 'lat')), may hold values from 0.25 to 4
- obs_count: int32 [2048], P(('mem', 'lat')), may hold values from 1 to 4096, 4194304 in all
- neighbours: int32 [2048, 6], P(('mem', 'lat')), may hold values from 0 to 47, as said below
- localization: float32 [2048, 6], P(('mem', 'lat')), may hold values from 0.2 to 1
Outputs:
- analysis: float32 [64, 16, 512, 256], P(None, None, ('mem', 'lat'))
The draws below stay inside these ranges and needn't reach their ends.
Inputs may be any that keep to these rules, and one draw needn't show every extreme that they name: The observations of a tile fill its first obs_count slots; later slots are ignored. `neighbours`: window index w names row group w % 16 of the strip w // 16 - 1 places east (strips wrap around). Entry 0 of each row is the tile itself; the others are distinct tiles of the previous, same or next row group in the previous, same or next strip.
All inputs are finite; a program needn't handle non-finite values. No bound on the sum of `obs_count` on one device may be relied on, other than what follows from the above.
Results may differ from the reference program's by a relative error of at most 0.0022.
Values may be sent and summed in bfloat16 or wider, within the bound.
No kernel may reach another device: no remote copies, remote signals or barrier semaphores. Data moves between devices by JAX's collectives and lax.ppermute only.
A program may use at most 256 MiB of HBM per device.

```python
import math
import jax
import jax.numpy as jnp
import numpy as np
from jax import lax

ENSEMBLE_SIZE = 64
CH = 16
NLON = 512
TILES_DEV = 16
OBS_CAP = 4096
NEIGH = 6
NS_ITERS = 5
NLAT = 256
TILES = 2048
TILE_ROWS = 16
LON_DEV = 4
DEVICES = 128


def draw_neighbours(key, part):
    key = jax.random.fold_in(key, 7)
    latitude_row_group = jnp.arange(TILES, dtype=jnp.int32) % TILES_DEV
    offsets = jnp.arange(9, dtype=jnp.int32)
    strip_step = offsets // 3 - 1
    row_step = offsets % 3 - 1
    destination_parallel = latitude_row_group[:, None] + row_step[None, :]
    inside = (destination_parallel >= 0) & (destination_parallel < TILES_DEV) & (offsets[None, :] != 4)
    scores = jax.random.randint(key, (TILES, 9), 0, 1 << 20, dtype=jnp.int32) * 16 + offsets[None, :]
    scores = jnp.where(inside, scores, -1)
    picked = lax.top_k(scores, NEIGH - 1)[1].astype(jnp.int32)
    window_index = (strip_step[picked] + 1) * TILES_DEV + latitude_row_group[:, None] + row_step[picked]
    self_index = TILES_DEV + latitude_row_group
    return jnp.concatenate([self_index[:, None], window_index], axis=1).astype(jnp.int32)


def level_of(rng, shape, shards, least, largest):
    def one(position, shards_of):
        heights = jax.random.uniform(jax.random.fold_in(jax.random.fold_in(rng, 6), position), (shards_of,), jnp.float32, least / len(shards), largest / len(shards))
        return jnp.repeat(jnp.exp(heights), shape[position] // shards_of).reshape((-1,) + (1,) * (len(shape) - position - 1))

    level = one(*shards[0])
    for cut in shards[1:]:
        level = level * one(*cut)
    return level


def profile(number_of, total, limit, skew):
    weights = [(1 << 20) // math.isqrt(standing ** skew) + 1 for standing in range(2, number_of + 1)]
    rest, given = total - limit - (number_of - 1), [1] * (number_of - 1)
    while rest > 0:
        movable = [i for i in range(number_of - 1) if given[i] < limit]
        pool, remaining = sum([weights[i] for i in movable]), rest
        for i in movable:
            more = min(limit - given[i], max(1, remaining * weights[i] // pool), rest)
            given[i] = given[i] + more
            rest = rest - more
    return np.array([limit] + given)


def ragged(key, count, total, reach, lean):
    if count == 2:
        one = jax.random.randint(key, (), max(1, total - reach), min(reach, total - 1) + 1)
        return jnp.stack([one, total - one])
    lengths = jnp.asarray(profile(count, total, reach, lean), jnp.int32)
    twos = (count - 1) // 2
    giver, sink = lengths[1:1 + 2 * twos:2], lengths[2:2 + 2 * twos:2]
    room = jnp.minimum(giver - 1, reach - sink)
    moved = jax.random.randint(jax.random.fold_in(key, 1), (twos,), 0, 1 << 20) % (room + 1)
    lengths = lengths.at[1:1 + 2 * twos:2].set(giver - moved).at[2:2 + 2 * twos:2].set(sink + moved)
    return lengths[jax.random.permutation(jax.random.fold_in(key, 2), count)]


def bell_draw(stream_key, extent, width, reach, pieces=(), held_as=jnp.bfloat16):
    gain = level_of(stream_key, extent, pieces, -0.22, 0.18) if pieces else 1.0
    array = jax.random.normal(stream_key, extent, jnp.float32) * width * gain
    return jnp.minimum(jnp.maximum(array, -reach), reach).astype(held_as)


def setup_inputs(seed: int = 0) -> dict:
    seeds = jax.random.split(jax.random.key(seed), 10)
    return {
        "prior_member_stack": bell_draw(seeds[0], (ENSEMBLE_SIZE, CH, NLAT, NLON), 1.0, 6.0, ((0, 4), (2, 32)), jnp.float32),
        "zonal_stability_ratio": jnp.clip(jax.random.uniform(seeds[1], (NLAT, NLON), jnp.float32, -0.45, 0.45) * level_of(seeds[1], (NLAT, NLON), ((0, 32),), -0.4, 0.0), -0.45, 0.45),
        "meridional_stability_ratio": jnp.clip(jax.random.uniform(seeds[2], (NLAT, NLON), jnp.float32, -0.45, 0.45) * level_of(seeds[2], (NLAT, NLON), ((0, 32),), -0.4, 0.0), -0.45, 0.45),
        "obs_perturb": bell_draw(seeds[3], (TILES, ENSEMBLE_SIZE, OBS_CAP), 0.3, 2.0, ((0, 128),)),
        "innovation": bell_draw(seeds[4], (TILES, OBS_CAP), 1.0, 6.0, ((0, 128),), jnp.float32),
        "inverse_error_variance": jnp.clip(jnp.exp(math.log(4.0) - 2.7725887 * jax.random.uniform(seeds[5], (TILES, OBS_CAP), jnp.float32) ** level_of(seeds[5], (TILES, OBS_CAP), ((0, 128),), -0.2, 0.2)), 0.25, 4.0),
        "obs_count": ragged(seeds[6], TILES, TILES * OBS_CAP // 2, OBS_CAP, 2).astype(jnp.int32),
        "neighbours": draw_neighbours(jax.random.fold_in(seeds[9], 71), 0),
        "localization": jnp.clip(jnp.exp(math.log(1.0) - 1.609438 * jax.random.uniform(seeds[8], (TILES, NEIGH), jnp.float32) ** level_of(seeds[8], (TILES, NEIGH), ((0, 128),), -0.2, 0.2)), 0.2, 1.0),
    }


def predict_model_state(prior_member_stack, zonal_stability_ratio, meridional_stability_ratio):
    east_neighbour = jnp.roll(prior_member_stack, -1, axis=-1)
    eastward_flux = jnp.maximum(zonal_stability_ratio, 0.0) * prior_member_stack + jnp.minimum(zonal_stability_ratio, 0.0) * east_neighbour
    divergence_x = eastward_flux - jnp.roll(eastward_flux, 1, axis=-1)
    zero_row = jnp.zeros(prior_member_stack.shape[:2] + (1, prior_member_stack.shape[3]), jnp.float32)
    fields_ext = jnp.concatenate([zero_row, prior_member_stack, zero_row], axis=2)
    north_ext = jnp.concatenate([jnp.zeros((1, meridional_stability_ratio.shape[1]), jnp.float32), meridional_stability_ratio], axis=0)
    flux_north = jnp.maximum(north_ext, 0.0) * fields_ext[:, :, :-1] + jnp.minimum(north_ext, 0.0) * fields_ext[:, :, 1:]
    return prior_member_stack - divergence_x - (flux_north[:, :, 1:] - flux_north[:, :, :-1])

def tile_terms(arrays):
    perturb, weight, drive = arrays
    weighted = (perturb.astype(jnp.float32) * weight.astype(jnp.float32)[:, None, :]).astype(jnp.bfloat16)
    gram_matrix = jnp.einsum('tko,tlo->tkl', weighted.astype(jnp.float32), perturb.astype(jnp.float32), precision=lax.Precision.HIGHEST)
    drive_vector = jnp.einsum('tko,to->tk', perturb.astype(jnp.float32), drive.astype(jnp.float32), precision=lax.Precision.HIGHEST)
    return (gram_matrix, drive_vector)

def transform_weights(curvature, drive_total, members):
    frob_scale = jnp.sqrt(lax.optimization_barrier(jnp.sum(curvature * curvature, axis=(1, 2))))
    identity = jnp.eye(members, dtype=jnp.float32)[None]
    current = curvature / frob_scale[:, None, None]
    inverse = jnp.broadcast_to(identity, curvature.shape)
    for _ in range(NS_ITERS):
        middle = 1.5 * identity - 0.5 * jnp.einsum('tij,tjk->tik', inverse, current, precision=lax.Precision.HIGHEST)
        current = jnp.einsum('tij,tjk->tik', current, middle, precision=lax.Precision.HIGHEST)
        inverse = jnp.einsum('tij,tjk->tik', middle, inverse, precision=lax.Precision.HIGHEST)
    spread_part = jnp.sqrt((members - 1.0) / frob_scale)[:, None, None] * inverse
    half_step = jnp.einsum('tij,tj->ti', inverse, drive_total, precision=lax.Precision.HIGHEST)
    ensemble_mean_portion = jnp.einsum('tij,tj->ti', inverse, half_step, precision=lax.Precision.HIGHEST) / frob_scale[:, None]
    return spread_part + ensemble_mean_portion[:, :, None]

def reference(prior_member_stack, zonal_stability_ratio, meridional_stability_ratio, obs_perturb, innovation, inverse_error_variance, obs_count, neighbours, localization):
    transported_quantities = predict_model_state(prior_member_stack, zonal_stability_ratio, meridional_stability_ratio)
    is_valid = jnp.arange(OBS_CAP, dtype=jnp.int32)[None, :] < obs_count[:, None]
    obs_weight = jnp.where(is_valid, inverse_error_variance, 0.0).astype(jnp.bfloat16)
    obs_drive = jnp.where(is_valid, inverse_error_variance * innovation, 0.0).astype(jnp.bfloat16)
    gram_matrix, drive_vector = lax.map(tile_terms, (obs_perturb.reshape(DEVICES, TILES_DEV, ENSEMBLE_SIZE, OBS_CAP), obs_weight.reshape(DEVICES, TILES_DEV, OBS_CAP), obs_drive.reshape(DEVICES, TILES_DEV, OBS_CAP)))
    gram_matrix = gram_matrix.reshape(TILES, ENSEMBLE_SIZE, ENSEMBLE_SIZE)
    drive_vector = drive_vector.reshape(TILES, ENSEMBLE_SIZE)
    strip_of = jnp.arange(TILES, dtype=jnp.int32) // TILES_DEV
    sources = (strip_of[:, None] + neighbours // TILES_DEV - 1) % DEVICES * TILES_DEV + neighbours % TILES_DEV
    sources = sources.astype(jnp.int32)
    curvature = jnp.broadcast_to((ENSEMBLE_SIZE - 1.0) * jnp.eye(ENSEMBLE_SIZE, dtype=jnp.float32), (TILES, ENSEMBLE_SIZE, ENSEMBLE_SIZE))
    drive_total = jnp.zeros((TILES, ENSEMBLE_SIZE), jnp.float32)
    for slot_index in range(NEIGH):
        curvature = curvature + localization[:, slot_index, None, None] * gram_matrix[sources[:, slot_index]]
        drive_total = drive_total + localization[:, slot_index, None] * drive_vector[sources[:, slot_index]]
    weights = transform_weights(curvature, drive_total, ENSEMBLE_SIZE)
    grid = jnp.transpose(transported_quantities, (0, 1, 3, 2)).reshape(ENSEMBLE_SIZE, CH, DEVICES, LON_DEV, TILES_DEV, TILE_ROWS)
    member_mean = lax.optimization_barrier(jnp.mean(grid, axis=0))
    anomaly = grid - member_mean
    update = jnp.einsum('icsxtr,stij->jcsxtr', anomaly, weights.reshape(DEVICES, TILES_DEV, ENSEMBLE_SIZE, ENSEMBLE_SIZE), precision=lax.Precision.HIGHEST)
    return (member_mean + update).reshape(ENSEMBLE_SIZE, CH, NLON, NLAT)
```

```python
import functools

import jax
import jax.numpy as jnp
from jax import lax
from jax.experimental import pallas as pl
from jax.experimental.pallas import tpu as pltpu
from jax.sharding import PartitionSpec as P

NS_ITERS = 5
LANES = 128
SUB = 8
VMEM_BYTES = 48 << 20


def call(kernel, name, out_shape, flops, traffic, **kw):
    return pl.pallas_call(
        kernel,
        name=name,
        out_shape=out_shape,
        cost_estimate=pl.CostEstimate(flops=flops, bytes_accessed=traffic, transcendentals=0),
        compiler_params=pltpu.CompilerParams(vmem_limit_bytes=VMEM_BYTES),
        **kw,
    )


def edge_rows(prior, north):
    rows, lon = prior.shape
    groups = rows // SUB

    def kernel(q_ref, v_ref, last_ref, first_ref):
        first_ref[...] = q_ref[pl.ds(0, groups, stride=SUB), :].astype(jnp.bfloat16)
        last_ref[0:groups, :] = q_ref[pl.ds(SUB - 1, groups, stride=SUB), :].astype(jnp.bfloat16)
        v = jnp.broadcast_to(v_ref[SUB - 1 : SUB, :], (16, LANES))
        high = v.astype(jnp.bfloat16).astype(jnp.float32)
        row = lax.broadcasted_iota(jnp.int32, (16, LANES), 0)
        parts = jnp.where(row == 0, high, jnp.where(row == 1, v - high, 0.0))
        last_ref[groups : groups + 16, :] = parts.astype(jnp.bfloat16)

    return call(
        kernel,
        "edge_rows",
        (
            jax.ShapeDtypeStruct((groups + 16, lon), jnp.bfloat16),
            jax.ShapeDtypeStruct((groups, lon), jnp.bfloat16),
        ),
        rows * lon,
        rows * lon * 4,
        grid=(lon // LANES,),
        in_specs=[
            pl.BlockSpec((rows, LANES), lambda s: (0, s)),
            pl.BlockSpec((SUB, LANES), lambda s: (0, s)),
        ],
        out_specs=(
            pl.BlockSpec((groups + 16, LANES), lambda s: (0, s)),
            pl.BlockSpec((groups, LANES), lambda s: (0, s)),
        ),
    )(prior, north)


def advect(prior, zonal, north, south_rows, north_rows, turn):
    members, channels, sub, lon = prior.shape
    steps = 4
    per_step = members // steps
    width = channels * sub
    blocks = lon // LANES

    def kernel(
        turn_ref, q_ref, u_ref, v_ref, vs_ref, hs_ref, hn_ref, out_ref, coef_ref, adv_ref, rows_ref
    ):
        step = pl.program_id(0)

        @pl.when(step == 0)
        def _():
            u, v = u_ref[...], v_ref[...]
            row = lax.broadcasted_iota(jnp.int32, (sub, lon), 0)
            below = vs_ref[0:1, :].astype(jnp.float32) + vs_ref[1:2, :].astype(jnp.float32)
            v_south = jnp.where(row == 0, jnp.broadcast_to(below, (sub, lon)), pltpu.roll(v, 1, 0))
            u_west = pltpu.roll(u, 1, 1)
            vp, vn = jnp.maximum(v, 0.0), jnp.minimum(v, 0.0)
            vps, vns = jnp.maximum(v_south, 0.0), jnp.minimum(v_south, 0.0)
            coef_ref[0] = (
                1.0 - jnp.maximum(u, 0.0) + jnp.minimum(u_west, 0.0) - vp + vns
            )
            coef_ref[1] = -jnp.minimum(u, 0.0)
            coef_ref[2] = jnp.maximum(u_west, 0.0)
            coef_ref[3] = jnp.where(row == sub - 1, 0.0, -vn)
            coef_ref[4] = jnp.where(row == 0, 0.0, vps)
            coef_ref[5] = jnp.broadcast_to(vps[0:1], (sub, lon))
            coef_ref[6] = jnp.broadcast_to(-vn[sub - 1 : sub], (sub, lon))

        shift = turn_ref[0] * sub
        for k in range(per_step):
            member = step * per_step + k
            for c in range(channels):
                q = q_ref[k, c]
                moved = (
                    q * coef_ref[0]
                    + pltpu.roll(q, lon - 1, 1) * coef_ref[1]
                    + pltpu.roll(q, 1, 1) * coef_ref[2]
                    + pltpu.roll(q, sub - 1, 0) * coef_ref[3]
                    + pltpu.roll(q, 1, 0) * coef_ref[4]
                )
                for b in range(blocks):
                    adv_ref[b, c * sub : (c + 1) * sub, :] = moved[:, b * LANES : (b + 1) * LANES]
            at = pl.ds(pl.multiple_of(k * channels, channels), channels)
            low = pl.ds(0, channels, stride=sub)
            high = pl.ds(sub - 1, channels, stride=sub)
            hs, hn = hs_ref[at, :].astype(jnp.float32), hn_ref[at, :].astype(jnp.float32)
            hs, hn = hs * coef_ref[5, 0:1], hn * coef_ref[6, 0:1]
            for b in range(blocks):
                lane = slice(b * LANES, (b + 1) * LANES)
                adv_ref[b, low, :] = adv_ref[b, low, :] + hs[:, lane]
                adv_ref[b, high, :] = adv_ref[b, high, :] + hn[:, lane]
                turned = pltpu.roll(adv_ref[b].T, shift, 1)
                rows_ref[pl.ds(b * LANES * members + member, LANES, stride=members), :] = turned

        @pl.when(step == steps - 1)
        def _():
            @pl.loop(0, lon // 32)
            def _(i):
                at = pl.ds(pl.multiple_of(i * 32 * members, 32 * members), 32 * members)
                out_ref[at, :] = rows_ref[at, :].astype(jnp.bfloat16)

    cells = members * channels * sub * lon
    return call(
        kernel,
        "advect",
        jax.ShapeDtypeStruct((lon * members, width), jnp.bfloat16),
        cells * 10,
        cells * 6,
        grid=(steps,),
        in_specs=[
            pl.BlockSpec(memory_space=pltpu.SMEM),
            pl.BlockSpec((per_step, channels, sub, lon), lambda s: (s, 0, 0, 0)),
            pl.BlockSpec((sub, lon), lambda s: (0, 0)),
            pl.BlockSpec((sub, lon), lambda s: (0, 0)),
            pl.BlockSpec((16, lon), lambda s: (members, 0)),
            pl.BlockSpec((per_step * channels, lon), lambda s: (s, 0)),
            pl.BlockSpec((per_step * channels, lon), lambda s: (s, 0)),
        ],
        out_specs=pl.BlockSpec((lon * members, width), lambda s: (0, 0)),
        scratch_shapes=[
            pltpu.VMEM((7, sub, lon), jnp.float32),
            pltpu.VMEM((blocks, width, LANES), jnp.float32),
            pltpu.VMEM((lon * members, width), jnp.float32),
        ],
    )(turn, prior, zonal, north, south_rows, south_rows, north_rows)


def tile_sums(perturb, innovation, inverse_error_variance, obs_count):
    tiles, members, cap = perturb.shape
    steps = 4
    per_step = tiles // steps
    half = members // 2

    def kernel(count_ref, p_ref, inn_ref, iev_ref, out_ref):
        step = pl.program_id(0)
        slot = lax.broadcasted_iota(jnp.int32, (1, cap), 1)
        for k in range(per_step):
            tile = step * per_step + k
            valid = slot < count_ref[tile]
            iev = iev_ref[pl.ds(tile, 1), :]
            weight = jnp.where(valid, iev, 0.0)
            drive = jnp.where(valid, iev * inn_ref[pl.ds(tile, 1), :], 0.0)
            weight = jnp.broadcast_to(weight, (16, cap)).astype(jnp.bfloat16)
            drive = jnp.broadcast_to(drive, (16, cap)).astype(jnp.bfloat16)
            p = p_ref[k]
            left = jnp.concatenate(
                [p[i * 16 : (i + 1) * 16] * weight for i in range(members // 16)] + [drive], axis=0
            )
            sums = lax.dot_general(
                left, p, (((1,), (1,)), ((), ())), preferred_element_type=jnp.float32
            )
            out_ref[k, 0:half, :] = jnp.concatenate([sums[0:half], sums[half:members]], axis=1)
            last = sums[members : members + SUB]
            out_ref[k, half : half + SUB, :] = jnp.concatenate([last, last], axis=1)

    return call(
        kernel,
        "tile_sums",
        jax.ShapeDtypeStruct((tiles, half + SUB, 2 * members), jnp.float32),
        2 * tiles * members * (members + 16) * cap,
        tiles * members * cap * 2,
        grid=(steps,),
        in_specs=[
            pl.BlockSpec(memory_space=pltpu.SMEM),
            pl.BlockSpec((per_step, members, cap), lambda s: (s, 0, 0)),
            pl.BlockSpec((tiles, cap), lambda s: (0, 0)),
            pl.BlockSpec((tiles, cap), lambda s: (0, 0)),
        ],
        out_specs=pl.BlockSpec((per_step, half + SUB, 2 * members), lambda s: (s, 0, 0)),
    )(obs_count, perturb, innovation, inverse_error_variance)


def transform(west, own, east, neighbours, localization):
    tiles, packed, lanes = own.shape
    members = lanes // 2
    half = members // 2
    neigh = neighbours.shape[1]
    dot = functools.partial(
        jnp.dot, precision=lax.Precision.HIGHEST, preferred_element_type=jnp.float32
    )

    def kernel(nb_ref, loc_ref, w_ref, o_ref, e_ref, out_ref, win_ref, cur_ref, inv_ref, mid_ref):
        win_ref[0:tiles] = w_ref[...]
        win_ref[tiles : 2 * tiles] = o_ref[...]
        win_ref[2 * tiles : 3 * tiles] = e_ref[...]
        row = lax.broadcasted_iota(jnp.int32, (members, members), 0)
        col = lax.broadcasted_iota(jnp.int32, (members, members), 1)
        eye = (row == col).astype(jnp.float32)
        drives, scales = [], []
        for t in range(tiles):
            total = loc_ref[t, 0] * win_ref[nb_ref[t, 0]]
            for n in range(1, neigh):
                total = total + loc_ref[t, n] * win_ref[nb_ref[t, n]]
            curvature = (members - 1.0) * eye + jnp.concatenate(
                [total[0:half, 0:members], total[0:half, members:]], axis=0
            )
            drives.append(total[half : half + SUB, 0:members])
            square = jnp.sum(curvature * curvature, axis=0, keepdims=True)
            scale = jnp.sqrt(jnp.sum(square, axis=1, keepdims=True))
            scales.append(scale)
            cur_ref[t] = curvature / scale
        for step in range(NS_ITERS):
            for t in range(tiles):
                product = cur_ref[t] if step == 0 else dot(inv_ref[t], cur_ref[t])
                mid_ref[t] = 1.5 * eye - 0.5 * product
            for t in range(tiles):
                middle = mid_ref[t]
                if step < NS_ITERS - 1:
                    cur_ref[t] = dot(cur_ref[t], middle)
                inv_ref[t] = middle if step == 0 else dot(middle, inv_ref[t])
        for t in range(tiles):
            flipped = inv_ref[t].T
            half_step = dot(drives[t], flipped)
            mean_part = dot(half_step, flipped)[0:1] / scales[t]
            weights = jnp.sqrt((members - 1.0) / scales[t]) * flipped + mean_part
            rest = (1.0 - jnp.sum(weights, axis=1, keepdims=True)) * (1.0 / members)
            weights = weights + rest
            high = weights.astype(jnp.bfloat16).astype(jnp.float32)
            out_ref[t] = jnp.concatenate([high, weights - high], axis=1).astype(jnp.bfloat16)

    cube = pltpu.VMEM((tiles, members, members), jnp.float32)
    vmem = pl.BlockSpec(memory_space=pltpu.VMEM)
    smem = pl.BlockSpec(memory_space=pltpu.SMEM)
    return call(
        kernel,
        "transform",
        jax.ShapeDtypeStruct((tiles, members, lanes), jnp.bfloat16),
        2 * tiles * members**3 * 72,
        tiles * packed * lanes * 12,
        in_specs=[smem, smem, vmem, vmem, vmem],
        out_specs=vmem,
        scratch_shapes=[pltpu.VMEM((3 * tiles, packed, lanes), jnp.float32), cube, cube, cube],
    )(neighbours, localization, west, own, east)


def analyse(arrived, weights, mem_count, lat_count, lon_strip):
    sources, rows, lanes = arrived.shape
    members_dev = rows // lon_strip
    tiles, members, _ = weights.shape
    bands = lat_count // tiles
    group = lanes // SUB
    halves = lat_count // group
    per_member = group * halves * lon_strip

    def kernel(a_ref, w_ref, out_ref, product_ref):
        x = pl.program_id(0)
        for g in range(tiles):
            block = jnp.concatenate(
                [
                    jnp.concatenate(
                        [a_ref[m * lat_count + g * bands + b] for m in range(mem_count)], axis=0
                    )
                    for b in range(bands)
                ],
                axis=1,
            )
            product = jnp.dot(
                w_ref[g],
                jnp.concatenate([block, block], axis=0),
                preferred_element_type=jnp.float32,
            )
            for b in range(bands):
                product_ref[g * bands + b] = product[:, b * lanes : (b + 1) * lanes]
        place = lax.broadcasted_iota(jnp.int32, (SUB, lanes), 1) // SUB

        @pl.loop(0, members // SUB)
        def _(j):
            at = pl.ds(pl.multiple_of(j * SUB, SUB), SUB)
            for half in range(halves):
                held = [product_ref[half * group + b, at, :] for b in range(group)]
                step = 1
                while step < group:
                    odd = (place // step) % 2 == 1
                    held = [
                        jnp.where(odd, held[(r + step) % group], held[r]) for r in range(group)
                    ]
                    step *= 2
                for c in range(group):
                    row = pltpu.roll(held[(-c) % group], (lanes - c * SUB) % lanes, 1)
                    first = j * SUB * per_member + (c * halves + half) * lon_strip + x
                    out_ref[pl.ds(first, SUB, stride=per_member), :] = row

    return call(
        kernel,
        "analyse",
        jax.ShapeDtypeStruct((members * per_member, lanes), jnp.float32),
        2 * tiles * members * 2 * members * bands * lanes * lon_strip,
        members * per_member * lanes * 6,
        grid=(lon_strip,),
        in_specs=[
            pl.BlockSpec((sources, members_dev, lanes), lambda x: (0, x, 0)),
            pl.BlockSpec((tiles, members, 2 * members), lambda x: (0, 0, 0)),
        ],
        out_specs=pl.BlockSpec((members * per_member, lanes), lambda x: (0, 0)),
        scratch_shapes=[pltpu.VMEM((lat_count, members, lanes), jnp.float32)],
    )(arrived, weights)


def per_device(
    prior_member_stack,
    zonal_stability_ratio,
    meridional_stability_ratio,
    obs_perturb,
    innovation,
    inverse_error_variance,
    obs_count,
    neighbours,
    localization,
):
    members_dev, channels, row_count, lon_count = prior_member_stack.shape
    mem_count, lat_count = lax.axis_size("mem"), lax.axis_size("lat")
    devices = mem_count * lat_count
    lon_strip = lon_count // devices
    members = members_dev * mem_count

    last, first = edge_rows(
        prior_member_stack.reshape(members_dev * channels * row_count, lon_count),
        meridional_stability_ratio,
    )
    up = [(i, i + 1) for i in range(lat_count - 1)]
    down = [(j, i) for i, j in up]
    south_rows = lax.ppermute(last, "lat", up)
    north_rows = lax.ppermute(first, "lat", down)

    sums = tile_sums(obs_perturb, innovation, inverse_error_variance, obs_count)
    ring = [(i, (i + 1) % devices) for i in range(devices)]
    both = ("mem", "lat")
    west = lax.ppermute(sums, both, ring)
    east = lax.ppermute(sums, both, [(j, i) for i, j in ring])

    turn = (lax.axis_index("lat") % (LANES // SUB)).astype(jnp.int32).reshape(1)
    sent = advect(
        prior_member_stack,
        zonal_stability_ratio,
        meridional_stability_ratio,
        south_rows,
        north_rows,
        turn,
    )
    sent = sent.reshape(devices, lon_strip * members_dev, channels * row_count)
    arrived = lax.all_to_all(sent, both, split_axis=0, concat_axis=0, tiled=True)
    weights = transform(west, sums, east, neighbours, localization)
    rows = analyse(arrived, weights, mem_count, lat_count, lon_strip)
    halves = lat_count * row_count // LANES
    out = rows.reshape(members, channels, halves, lon_strip, LANES)
    out = jnp.transpose(out, (0, 1, 3, 2, 4))
    return out.reshape(members, channels, lon_strip, lat_count * row_count)


def solution(mesh):
    in_specs = (
        P("mem", None, "lat", None),
        P("lat", None),
        P("lat", None),
        P(("mem", "lat"), None, None),
        P(("mem", "lat"), None),
        P(("mem", "lat"), None),
        P(("mem", "lat")),
        P(("mem", "lat"), None),
        P(("mem", "lat"), None),
    )
    out_specs = P(None, None, ("mem", "lat"), None)
    return jax.shard_map(
        per_device, mesh=mesh, in_specs=in_specs, out_specs=out_specs, check_vma=False
    )
```

```python
import functools

import jax
import jax.numpy as jnp
from jax import lax
from jax.experimental import pallas as pl
from jax.experimental.pallas import tpu as pltpu
from jax.sharding import PartitionSpec as P

NS_ITERS = 5
LANES = 128
SUB = 8


def call(kernel, name, out_shape, flops, traffic, vmem=24, **kw):
    return pl.pallas_call(
        kernel,
        name=name,
        out_shape=out_shape,
        cost_estimate=pl.CostEstimate(flops=flops, bytes_accessed=traffic, transcendentals=0),
        compiler_params=pltpu.CompilerParams(vmem_limit_bytes=vmem << 20),
        **kw,
    )


def parity():
    return lax.rem(lax.axis_index("lat"), 2)


def edge_rows(prior, north):
    groups, sub, lon = prior.shape

    def kernel(q_ref, v_ref, first_ref, second_ref, north_ref, rows_ref, sem):
        odd = parity()
        copies = [
            pltpu.make_async_copy(q_ref.at[:, (sub - 1) * side, :], rows_ref.at[k], sem.at[k])
            for k, side in enumerate((1 - odd, odd))
        ]
        courant = pltpu.make_async_copy(v_ref, north_ref, sem.at[2])
        courant.start()
        for copy in copies:
            copy.start()
        courant.wait()
        v = jnp.broadcast_to(north_ref[sub - 1 : sub, :], (16, lon))
        high = v.astype(jnp.bfloat16).astype(jnp.float32)
        row = lax.broadcasted_iota(jnp.int32, (16, lon), 0)
        parts = jnp.where(row == 0, high, jnp.where(row == 1, v - high, 0.0)).astype(jnp.bfloat16)
        for k, ref in enumerate((first_ref, second_ref)):
            copies[k].wait()
            ref[0:groups, :] = rows_ref[k].astype(jnp.bfloat16)
            ref[groups : groups + 16, :] = parts

    out = jax.ShapeDtypeStruct((groups + 16, lon), jnp.bfloat16)
    vmem = pl.BlockSpec(memory_space=pltpu.VMEM)
    return call(
        kernel,
        "edge_rows",
        (out, out),
        groups * lon * 2,
        groups * lon * 12,
        vmem=52,
        in_specs=[pl.BlockSpec(memory_space=pl.ANY)] * 2,
        out_specs=(vmem, vmem),
        scratch_shapes=[
            pltpu.VMEM((sub, lon), jnp.float32),
            pltpu.VMEM((2, groups, lon), jnp.float32),
            pltpu.SemaphoreType.DMA((3,)),
        ],
    )(prior, north)


def advect(prior, zonal, north, first_rows, second_rows, members, channels):
    sub, lon = zonal.shape
    blocks = lon // LANES
    width = channels * sub
    edges = members * channels
    chunks = 4
    chunk = lon * members // chunks
    starts = (0, members // 8, members // 2)
    ends = starts[1:] + (members,)

    def kernel(
        q_hbm, u_ref, v_ref, ra_ref, rb_ref, out_ref,
        q_ref, coef_ref, halo_ref, adv_ref, rows_ref, sent_ref, in_sem, out_sem,
    ):
        def copy_in(group, b):
            some = pl.ds(starts[group], ends[group] - starts[group])
            return pltpu.make_async_copy(
                q_hbm.at[some, :, pl.ds(b * LANES, LANES)],
                q_ref.at[b, some, pl.ds(sub, width)],
                in_sem.at[group, b],
            )

        for group in range(len(starts)):
            for b in range(blocks):
                copy_in(group, b).start()

        odd = parity()
        u, v = u_ref[...], v_ref[...]
        row = lax.broadcasted_iota(jnp.int32, (sub, lon), 0)
        below = [ref[edges : edges + 16, :].astype(jnp.float32) for ref in (ra_ref, rb_ref)]
        below = jnp.where(odd == 1, below[0], below[1])
        below = jnp.broadcast_to(below[0:1] + below[1:2], (sub, lon))
        v_south = jnp.where(row == 0, below, pltpu.roll(v, 1, 0))
        u_west = pltpu.roll(u, 1, 1)
        vp, vn = jnp.maximum(v, 0.0), jnp.minimum(v, 0.0)
        vps, vns = jnp.maximum(v_south, 0.0), jnp.minimum(v_south, 0.0)
        coefs = (
            1.0 - jnp.maximum(u, 0.0) + jnp.minimum(u_west, 0.0) - vp + vns,
            -jnp.minimum(u, 0.0),
            jnp.maximum(u_west, 0.0),
            -vn,
            vps,
        )
        for k, coef in enumerate(coefs):
            for b in range(blocks):
                coef_ref[k, b] = coef[:, b * LANES : (b + 1) * LANES]
        lane = lax.broadcasted_iota(jnp.int32, (sub, LANES), 1)
        line = lax.broadcasted_iota(jnp.int32, (sub, LANES), 0)
        start = channels - lax.rem(lax.axis_index("lat"), channels)

        def stencil(member, slot):
            at = pl.ds(pl.multiple_of(member * channels, channels), channels)
            for k, ref in enumerate((ra_ref, rb_ref)):
                halo = ref[at, :].astype(jnp.float32)
                for b in range(blocks):
                    halo_ref[slot, k, b] = halo[:, b * LANES : (b + 1) * LANES]
            coef = [[coef_ref[k, b] for b in range(blocks)] for k in range(5)]
            for p in range(channels):
                c = lax.rem(start + p, channels)
                base = pl.multiple_of((c + 1) * sub, sub)
                q = [q_ref[b, member, pl.ds(base, sub), :] for b in range(blocks)]
                east = [pltpu.roll(x, LANES - 1, 1) for x in q]
                west = [pltpu.roll(x, 1, 1) for x in q]
                for b in range(blocks):
                    q_east = jnp.where(lane == LANES - 1, east[(b + 1) % blocks], east[b])
                    q_west = jnp.where(lane == 0, west[b - 1], west[b])
                    q_north = q_ref[b, member, pl.ds(base + 1, sub), :]
                    q_south = q_ref[b, member, pl.ds(base - 1, sub), :]
                    halo_south = halo_ref[slot, 1 - odd, b, pl.ds(c, 1), :]
                    halo_north = halo_ref[slot, odd, b, pl.ds(c, 1), :]
                    q_south = jnp.where(line == 0, halo_south, q_south)
                    q_north = jnp.where(line == sub - 1, halo_north, q_north)
                    adv_ref[slot, b, p * sub : (p + 1) * sub, :] = (
                        q[b] * coef[0][b]
                        + q_east * coef[1][b]
                        + q_west * coef[2][b]
                        + q_north * coef[3][b]
                        + q_south * coef[4][b]
                    )

        def flush(member, slot):
            for b in range(blocks):
                first = b * LANES * members + member
                rows_ref[pl.ds(first, LANES, stride=members), :] = adv_ref[slot, b].T

        @pl.loop(0, members // 2)
        def _(pair):
            for group, first in enumerate(starts):

                @pl.when(pair == first // 2)
                def _():
                    for b in range(blocks):
                        copy_in(group, b).wait()

            member = pair * 2
            stencil(member, 0)
            flush(lax.rem(member + members - 1, members), 1)
            stencil(member + 1, 1)
            flush(member, 0)

        flush(members - 1, 1)

        copies = []
        for i in range(chunks):
            at = pl.ds(i * chunk, chunk)

            @pl.loop(0, chunk // 512)
            def _(j):
                part = pl.ds(pl.multiple_of(i * chunk + j * 512, 512), 512)
                sent_ref[part, :] = rows_ref[part, :].astype(jnp.bfloat16)

            copies.append(pltpu.make_async_copy(sent_ref.at[at], out_ref.at[at], out_sem.at[i]))
            copies[-1].start()
        for copy in copies:
            copy.wait()

    cells = members * channels * sub * lon
    vmem = pl.BlockSpec(memory_space=pltpu.VMEM)
    hbm = pl.BlockSpec(memory_space=pl.ANY)
    return call(
        kernel,
        "advect",
        jax.ShapeDtypeStruct((lon * members, width), jnp.bfloat16),
        cells * 10,
        cells * 6,
        vmem=52,
        in_specs=[hbm] + [vmem] * 4,
        out_specs=hbm,
        scratch_shapes=[
            pltpu.VMEM((blocks, members, width + 2 * sub, LANES), jnp.float32),
            pltpu.VMEM((5, blocks, sub, LANES), jnp.float32),
            pltpu.VMEM((2, 2, blocks, channels, LANES), jnp.float32),
            pltpu.VMEM((2, blocks, width, LANES), jnp.float32),
            pltpu.VMEM((lon * members, width), jnp.float32),
            pltpu.VMEM((lon * members, width), jnp.bfloat16),
            pltpu.SemaphoreType.DMA((len(starts), blocks)),
            pltpu.SemaphoreType.DMA((chunks,)),
        ],
    )(prior, zonal, north, first_rows, second_rows)


def tile_sums(perturb, innovation, inverse_error_variance, obs_count):
    tiles, members, cap = perturb.shape
    half = members // 2
    parts = 4
    per_part = tiles // parts

    def kernel(count_ref, p_ref, inn_ref, iev_ref, out_ref, held_ref, sem):
        copies = [
            pltpu.make_async_copy(
                p_ref.at[pl.ds(i * per_part, per_part)],
                held_ref.at[pl.ds(i * per_part, per_part)],
                sem.at[i],
            )
            for i in range(parts)
        ]
        for copy in copies:
            copy.start()
        slot = lax.broadcasted_iota(jnp.int32, (1, cap), 1)
        for tile in range(tiles):
            if tile % per_part == 0:
                copies[tile // per_part].wait()
            valid = slot < count_ref[tile]
            iev = iev_ref[tile : tile + 1, :]
            weight = jnp.where(valid, iev, 0.0)
            drive = jnp.where(valid, iev * inn_ref[tile : tile + 1, :], 0.0)
            weight = jnp.broadcast_to(weight, (16, cap)).astype(jnp.bfloat16)
            drive = jnp.broadcast_to(drive, (16, cap)).astype(jnp.bfloat16)
            p = held_ref[tile]
            left = jnp.concatenate(
                [p[i * 16 : (i + 1) * 16] * weight for i in range(members // 16)] + [drive], axis=0
            )
            sums = lax.dot_general(
                left, p, (((1,), (1,)), ((), ())), preferred_element_type=jnp.float32
            )
            out_ref[tile, 0:half, :] = jnp.concatenate([sums[0:half], sums[half:members]], axis=1)
            last = sums[members : members + SUB]
            out_ref[tile, half : half + SUB, :] = jnp.concatenate([last, last], axis=1)

    vmem = pl.BlockSpec(memory_space=pltpu.VMEM)
    return call(
        kernel,
        "tile_sums",
        jax.ShapeDtypeStruct((tiles, half + SUB, 2 * members), jnp.float32),
        2 * tiles * members * (members + 16) * cap,
        tiles * members * cap * 2,
        vmem=50,
        in_specs=[
            pl.BlockSpec(memory_space=pltpu.SMEM),
            pl.BlockSpec(memory_space=pl.ANY),
            vmem,
            vmem,
        ],
        out_specs=vmem,
        scratch_shapes=[
            pltpu.VMEM((tiles, members, cap), jnp.bfloat16),
            pltpu.SemaphoreType.DMA((parts,)),
        ],
    )(obs_count, perturb, innovation, inverse_error_variance)


def transform(own, first, second, neighbours, localization):
    tiles, packed, lanes = own.shape
    members = lanes // 2
    half = members // 2
    neigh = neighbours.shape[1]
    dot = functools.partial(
        jnp.dot, precision=lax.Precision.HIGHEST, preferred_element_type=jnp.float32
    )

    def kernel(nb_ref, loc_ref, o_ref, a_ref, b_ref, out_ref, win_ref, cur_ref, inv_ref, mid_ref):
        odd = parity()
        win_ref[tiles : 2 * tiles] = o_ref[...]
        win_ref[pl.ds((1 - odd) * 2 * tiles, tiles)] = a_ref[...]
        win_ref[pl.ds(odd * 2 * tiles, tiles)] = b_ref[...]
        row = lax.broadcasted_iota(jnp.int32, (members, members), 0)
        col = lax.broadcasted_iota(jnp.int32, (members, members), 1)
        eye = (row == col).astype(jnp.float32)
        drives, scales = [], []
        for t in range(tiles):
            total = loc_ref[t, 0] * win_ref[nb_ref[t, 0]]
            for n in range(1, neigh):
                total = total + loc_ref[t, n] * win_ref[nb_ref[t, n]]
            curvature = (members - 1.0) * eye + jnp.concatenate(
                [total[0:half, 0:members], total[0:half, members:]], axis=0
            )
            drives.append(total[half : half + SUB, 0:members])
            square = jnp.sum(curvature * curvature, axis=0, keepdims=True)
            scale = jnp.sqrt(jnp.sum(square, axis=1, keepdims=True))
            scales.append(scale)
            cur_ref[t] = curvature / scale
        for step in range(NS_ITERS):
            for t in range(tiles):
                product = cur_ref[t] if step == 0 else dot(inv_ref[t], cur_ref[t])
                mid_ref[t] = 1.5 * eye - 0.5 * product
            for t in range(tiles):
                middle = mid_ref[t]
                if step < NS_ITERS - 1:
                    cur_ref[t] = dot(cur_ref[t], middle)
                inv_ref[t] = middle if step == 0 else dot(middle, inv_ref[t])
        for t in range(tiles):
            flipped = inv_ref[t].T
            half_step = dot(drives[t], flipped)
            mean_part = dot(half_step, flipped)[0:1] / scales[t]
            weights = jnp.sqrt((members - 1.0) / scales[t]) * flipped + mean_part
            rest = (1.0 - jnp.sum(weights, axis=1, keepdims=True)) * (1.0 / members)
            weights = weights + rest
            high = weights.astype(jnp.bfloat16).astype(jnp.float32)
            out_ref[t] = jnp.concatenate([high, weights - high], axis=1).astype(jnp.bfloat16)

    cube = pltpu.VMEM((tiles, members, members), jnp.float32)
    vmem = pl.BlockSpec(memory_space=pltpu.VMEM)
    smem = pl.BlockSpec(memory_space=pltpu.SMEM)
    return call(
        kernel,
        "transform",
        jax.ShapeDtypeStruct((tiles, members, lanes), jnp.bfloat16),
        2 * tiles * members**3 * 72,
        tiles * packed * lanes * 12,
        in_specs=[smem, smem, vmem, vmem, vmem],
        out_specs=vmem,
        scratch_shapes=[pltpu.VMEM((3 * tiles, packed, lanes), jnp.float32), cube, cube, cube],
    )(neighbours, localization, own, first, second)


def analyse(arrived, weights, mem_count, lat_count, lon_strip):
    sources, rows, lanes = arrived.shape
    members_dev = rows // lon_strip
    tiles, members, _ = weights.shape
    bands = lat_count // tiles
    group = lanes // SUB
    halves = lat_count // group
    per_member = group * halves * lon_strip
    chunks = members // SUB
    chunk_rows = SUB * per_member

    def kernel(a_ref, w_ref, out_ref, product_ref, rows_ref, sem):
        @pl.loop(0, lon_strip)
        def _(x):
            at = pl.ds(pl.multiple_of(x * members_dev, members_dev), members_dev)
            for g in range(tiles):
                block = jnp.concatenate(
                    [
                        jnp.concatenate(
                            [a_ref[m * lat_count + g * bands + b, at, :] for m in range(mem_count)],
                            axis=0,
                        )
                        for b in range(bands)
                    ],
                    axis=1,
                )
                product = jnp.dot(
                    w_ref[g],
                    jnp.concatenate([block, block], axis=0),
                    preferred_element_type=jnp.float32,
                )
                for b in range(bands):
                    product_ref[x, g * bands + b] = product[:, b * lanes : (b + 1) * lanes]

        place = lax.broadcasted_iota(jnp.int32, (SUB, lanes), 1) // SUB

        def copy_out(j):
            at = pl.ds(pl.multiple_of(j * chunk_rows, chunk_rows), chunk_rows)
            return pltpu.make_async_copy(rows_ref.at[at], out_ref.at[at], sem.at[j])

        @pl.loop(0, chunks)
        def _(j):
            at = pl.ds(pl.multiple_of(j * SUB, SUB), SUB)
            for x in range(lon_strip):
                for half in range(halves):
                    held = [product_ref[x, half * group + b, at, :] for b in range(group)]
                    step = 1
                    while step < group:
                        odd = (place // step) % 2 == 1
                        held = [
                            jnp.where(odd, held[(r + step) % group], held[r]) for r in range(group)
                        ]
                        step *= 2
                    for c in range(group):
                        row = pltpu.roll(held[(-c) % group], (lanes - c * SUB) % lanes, 1)
                        first = j * chunk_rows + (c * halves + half) * lon_strip + x
                        rows_ref[pl.ds(first, SUB, stride=per_member), :] = row
            copy_out(j).start()

        @pl.loop(0, chunks)
        def _(j):
            copy_out(j).wait()

    vmem = pl.BlockSpec(memory_space=pltpu.VMEM)
    return call(
        kernel,
        "analyse",
        jax.ShapeDtypeStruct((members * per_member, lanes), jnp.float32),
        2 * tiles * members * 2 * members * bands * lanes * lon_strip,
        members * per_member * lanes * 6,
        in_specs=[vmem, vmem],
        out_specs=pl.BlockSpec(memory_space=pl.ANY),
        scratch_shapes=[
            pltpu.VMEM((lon_strip, lat_count, members, lanes), jnp.float32),
            pltpu.VMEM((members * per_member, lanes), jnp.float32),
            pltpu.SemaphoreType.DMA((chunks,)),
        ],
    )(arrived, weights)


def per_device(
    prior_member_stack,
    zonal_stability_ratio,
    meridional_stability_ratio,
    obs_perturb,
    innovation,
    inverse_error_variance,
    obs_count,
    neighbours,
    localization,
):
    members_dev, channels, row_count, lon_count = prior_member_stack.shape
    mem_count, lat_count = lax.axis_size("mem"), lax.axis_size("lat")
    devices = mem_count * lat_count
    lon_strip = lon_count // devices
    members = members_dev * mem_count

    first_rows, second_rows = edge_rows(
        prior_member_stack.reshape(members_dev * channels, row_count, lon_count),
        meridional_stability_ratio,
    )

    def swap(first, count, ring):
        pairs = [(i, (i + 1) % count) for i in range(first, count if ring else count - 1, 2)]
        return pairs + [(j, i) for i, j in pairs]

    first_rows = lax.ppermute(first_rows, "lat", swap(0, lat_count, False))
    second_rows = lax.ppermute(second_rows, "lat", swap(1, lat_count, False))

    sums = tile_sums(obs_perturb, innovation, inverse_error_variance, obs_count)
    first_rows, second_rows, sums = lax.optimization_barrier((first_rows, second_rows, sums))
    both = ("mem", "lat")
    first_sums = lax.ppermute(sums, both, swap(0, devices, True))
    second_sums = lax.ppermute(sums, both, swap(1, devices, True))

    sent = advect(
        prior_member_stack.reshape(members_dev, channels * row_count, lon_count),
        zonal_stability_ratio,
        meridional_stability_ratio,
        first_rows,
        second_rows,
        members_dev,
        channels,
    )
    sent = sent.reshape(devices, lon_strip * members_dev, channels * row_count)
    sent, first_sums, second_sums = lax.optimization_barrier((sent, first_sums, second_sums))
    arrived = lax.all_to_all(sent, both, split_axis=0, concat_axis=0, tiled=True)
    weights = transform(sums, first_sums, second_sums, neighbours, localization)
    rows = analyse(arrived, weights, mem_count, lat_count, lon_strip)
    halves = lat_count * row_count // LANES
    out = rows.reshape(members, channels, halves, lon_strip, LANES)
    out = jnp.transpose(out, (0, 1, 3, 2, 4))
    return out.reshape(members, channels, lon_strip, lat_count * row_count)


def solution(mesh):
    in_specs = (
        P("mem", None, "lat", None),
        P("lat", None),
        P("lat", None),
        P(("mem", "lat"), None, None),
        P(("mem", "lat"), None),
        P(("mem", "lat"), None),
        P(("mem", "lat")),
        P(("mem", "lat"), None),
        P(("mem", "lat"), None),
    )
    out_specs = P(None, None, ("mem", "lat"), None)
    return jax.shard_map(
        per_device, mesh=mesh, in_specs=in_specs, out_specs=out_specs, check_vma=False
    )
```

```python
import functools

import jax
import jax.numpy as jnp
from jax import lax
from jax.experimental import pallas as pl
from jax.experimental.pallas import tpu as pltpu
from jax.sharding import PartitionSpec as P

NS_ITERS = 5
LANES = 128
SUB = 8


def call(kernel, name, out_shape, flops, traffic, vmem=24, **kw):
    return pl.pallas_call(
        kernel,
        name=name,
        out_shape=out_shape,
        cost_estimate=pl.CostEstimate(flops=flops, bytes_accessed=traffic, transcendentals=0),
        compiler_params=pltpu.CompilerParams(vmem_limit_bytes=vmem << 20),
        **kw,
    )


def parity():
    return lax.rem(lax.axis_index("lat"), 2)


def edge_rows(prior, north):
    groups, sub, lon = prior.shape

    def kernel(q_ref, v_ref, first_ref, second_ref, north_ref, rows_ref, sem):
        odd = parity()
        copies = [
            pltpu.make_async_copy(q_ref.at[:, (sub - 1) * side, :], rows_ref.at[k], sem.at[k])
            for k, side in enumerate((1 - odd, odd))
        ]
        courant = pltpu.make_async_copy(v_ref, north_ref, sem.at[2])
        courant.start()
        for copy in copies:
            copy.start()
        courant.wait()
        v = jnp.broadcast_to(north_ref[sub - 1 : sub, :], (16, lon))
        high = v.astype(jnp.bfloat16).astype(jnp.float32)
        row = lax.broadcasted_iota(jnp.int32, (16, lon), 0)
        parts = jnp.where(row == 0, high, jnp.where(row == 1, v - high, 0.0)).astype(jnp.bfloat16)
        for k, ref in enumerate((first_ref, second_ref)):
            copies[k].wait()
            ref[0:groups, :] = rows_ref[k].astype(jnp.bfloat16)
            ref[groups : groups + 16, :] = parts

    out = jax.ShapeDtypeStruct((groups + 16, lon), jnp.bfloat16)
    vmem = pl.BlockSpec(memory_space=pltpu.VMEM)
    return call(
        kernel,
        "edge_rows",
        (out, out),
        groups * lon * 2,
        groups * lon * 12,
        vmem=52,
        in_specs=[pl.BlockSpec(memory_space=pl.ANY)] * 2,
        out_specs=(vmem, vmem),
        scratch_shapes=[
            pltpu.VMEM((sub, lon), jnp.float32),
            pltpu.VMEM((2, groups, lon), jnp.float32),
            pltpu.SemaphoreType.DMA((3,)),
        ],
    )(prior, north)


def advect(prior, zonal, north, first_rows, second_rows, members, channels):
    sub, lon = zonal.shape
    blocks = lon // LANES
    width = channels * sub
    edges = members * channels
    chunk = LANES * members
    pitch = members + SUB
    starts = (0, members // 4, members // 2)
    ends = starts[1:] + (members,)

    def kernel(
        q_hbm, u_ref, v_ref, ra_ref, rb_ref, out_ref,
        q_ref, coef_ref, halo_ref, adv_ref, rows_ref, sent_ref, in_sem, out_sem,
    ):
        def copy_in(group, b):
            some = pl.ds(starts[group], ends[group] - starts[group])
            return pltpu.make_async_copy(
                q_hbm.at[some, :, pl.ds(b * LANES, LANES)],
                q_ref.at[b, some, pl.ds(sub, width)],
                in_sem.at[group, b],
            )

        for group in range(len(starts)):
            for b in range(blocks):
                copy_in(group, b).start()

        odd = parity()
        u, v = u_ref[...], v_ref[...]
        row = lax.broadcasted_iota(jnp.int32, (sub, lon), 0)
        below = [ref[edges : edges + 16, :].astype(jnp.float32) for ref in (ra_ref, rb_ref)]
        below = jnp.where(odd == 1, below[0], below[1])
        below = jnp.broadcast_to(below[0:1] + below[1:2], (sub, lon))
        v_south = jnp.where(row == 0, below, pltpu.roll(v, 1, 0))
        u_west = pltpu.roll(u, 1, 1)
        vp, vn = jnp.maximum(v, 0.0), jnp.minimum(v, 0.0)
        vps, vns = jnp.maximum(v_south, 0.0), jnp.minimum(v_south, 0.0)
        coefs = (
            1.0 - jnp.maximum(u, 0.0) + jnp.minimum(u_west, 0.0) - vp + vns,
            -jnp.minimum(u, 0.0),
            jnp.maximum(u_west, 0.0),
            -vn,
            vps,
        )
        for k, coef in enumerate(coefs):
            for b in range(blocks):
                coef_ref[k, b] = coef[:, b * LANES : (b + 1) * LANES]
        lane = lax.broadcasted_iota(jnp.int32, (sub, LANES), 1)
        line = lax.broadcasted_iota(jnp.int32, (sub, LANES), 0)
        start = channels - lax.rem(lax.axis_index("lat"), channels)

        def stencil(member, slot):
            at = pl.ds(pl.multiple_of(member * channels, channels), channels)
            for k, ref in enumerate((ra_ref, rb_ref)):
                halo = ref[at, :].astype(jnp.float32)
                for b in range(blocks):
                    halo_ref[slot, k, b] = halo[:, b * LANES : (b + 1) * LANES]
            coef = [[coef_ref[k, b] for b in range(blocks)] for k in range(5)]
            for p in range(channels):
                c = lax.rem(start + p, channels)
                base = pl.multiple_of((c + 1) * sub, sub)
                q = [q_ref[b, member, pl.ds(base, sub), :] for b in range(blocks)]
                east = [pltpu.roll(x, LANES - 1, 1) for x in q]
                west = [pltpu.roll(x, 1, 1) for x in q]
                for b in range(blocks):
                    q_east = jnp.where(lane == LANES - 1, east[(b + 1) % blocks], east[b])
                    q_west = jnp.where(lane == 0, west[b - 1], west[b])
                    q_north = q_ref[b, member, pl.ds(base + 1, sub), :]
                    q_south = q_ref[b, member, pl.ds(base - 1, sub), :]
                    halo_south = halo_ref[slot, 1 - odd, b, pl.ds(c, 1), :]
                    halo_north = halo_ref[slot, odd, b, pl.ds(c, 1), :]
                    q_south = jnp.where(line == 0, halo_south, q_south)
                    q_north = jnp.where(line == sub - 1, halo_north, q_north)
                    adv_ref[member, b, p * sub : (p + 1) * sub, :] = (
                        q[b] * coef[0][b]
                        + q_east * coef[1][b]
                        + q_west * coef[2][b]
                        + q_north * coef[3][b]
                        + q_south * coef[4][b]
                    )

        @pl.loop(0, members // 4)
        def _(four):
            for group, first in enumerate(starts):

                @pl.when(four == first // 4)
                def _():
                    for b in range(blocks):
                        copy_in(group, b).wait()

            for k in range(4):
                stencil(four * 4 + k, k)

        copies = []
        for b in range(blocks):
            for member in range(members):
                at = pl.ds(member, LANES, stride=pitch)
                rows_ref[b % 2, at, :] = adv_ref[member, b].T
            for x in range(LANES):
                to = pl.ds(b * chunk + x * members, members)
                at = pl.ds(x * pitch, members)
                sent_ref[to, :] = rows_ref[b % 2, at, :].astype(jnp.bfloat16)
            at = pl.ds(b * chunk, chunk)
            copies.append(pltpu.make_async_copy(sent_ref.at[at], out_ref.at[at], out_sem.at[b]))
            copies[-1].start()
        for copy in copies:
            copy.wait()

    cells = members * channels * sub * lon
    vmem = pl.BlockSpec(memory_space=pltpu.VMEM)
    hbm = pl.BlockSpec(memory_space=pl.ANY)
    return call(
        kernel,
        "advect",
        jax.ShapeDtypeStruct((lon * members, width), jnp.bfloat16),
        cells * 10,
        cells * 6,
        vmem=52,
        in_specs=[hbm] + [vmem] * 4,
        out_specs=hbm,
        scratch_shapes=[
            pltpu.VMEM((blocks, members, width + 2 * sub, LANES), jnp.float32),
            pltpu.VMEM((5, blocks, sub, LANES), jnp.float32),
            pltpu.VMEM((4, 2, blocks, channels, LANES), jnp.float32),
            pltpu.VMEM((members, blocks, width, LANES), jnp.float32),
            pltpu.VMEM((2, LANES * pitch, width), jnp.float32),
            pltpu.VMEM((lon * members, width), jnp.bfloat16),
            pltpu.SemaphoreType.DMA((len(starts), blocks)),
            pltpu.SemaphoreType.DMA((blocks,)),
        ],
    )(prior, zonal, north, first_rows, second_rows)


def tile_sums(perturb, innovation, inverse_error_variance, obs_count):
    tiles, members, cap = perturb.shape
    half = members // 2
    parts = 4
    per_part = tiles // parts

    def kernel(count_ref, p_ref, inn_ref, iev_ref, out_ref, held_ref, sem):
        copies = [
            pltpu.make_async_copy(
                p_ref.at[pl.ds(i * per_part, per_part)],
                held_ref.at[pl.ds(i * per_part, per_part)],
                sem.at[i],
            )
            for i in range(parts)
        ]
        for copy in copies:
            copy.start()
        slot = lax.broadcasted_iota(jnp.int32, (1, cap), 1)
        for tile in range(tiles):
            if tile % per_part == 0:
                copies[tile // per_part].wait()
            valid = slot < count_ref[tile]
            iev = iev_ref[tile : tile + 1, :]
            weight = jnp.where(valid, iev, 0.0)
            drive = jnp.where(valid, iev * inn_ref[tile : tile + 1, :], 0.0)
            weight = jnp.broadcast_to(weight, (16, cap)).astype(jnp.bfloat16)
            drive = jnp.broadcast_to(drive, (16, cap)).astype(jnp.bfloat16)
            p = held_ref[tile]
            left = jnp.concatenate(
                [p[i * 16 : (i + 1) * 16] * weight for i in range(members // 16)] + [drive], axis=0
            )
            sums = lax.dot_general(
                left, p, (((1,), (1,)), ((), ())), preferred_element_type=jnp.float32
            )
            out_ref[tile, 0:half, :] = jnp.concatenate([sums[0:half], sums[half:members]], axis=1)
            last = sums[members : members + SUB]
            out_ref[tile, half : half + SUB, :] = jnp.concatenate([last, last], axis=1)

    vmem = pl.BlockSpec(memory_space=pltpu.VMEM)
    return call(
        kernel,
        "tile_sums",
        jax.ShapeDtypeStruct((tiles, half + SUB, 2 * members), jnp.float32),
        2 * tiles * members * (members + 16) * cap,
        tiles * members * cap * 2,
        vmem=50,
        in_specs=[
            pl.BlockSpec(memory_space=pltpu.SMEM),
            pl.BlockSpec(memory_space=pl.ANY),
            vmem,
            vmem,
        ],
        out_specs=vmem,
        scratch_shapes=[
            pltpu.VMEM((tiles, members, cap), jnp.bfloat16),
            pltpu.SemaphoreType.DMA((parts,)),
        ],
    )(obs_count, perturb, innovation, inverse_error_variance)


def transform(own, first, second, neighbours, localization):
    tiles, packed, lanes = own.shape
    members = lanes // 2
    half = members // 2
    neigh = neighbours.shape[1]
    dot = functools.partial(
        jnp.dot, precision=lax.Precision.HIGHEST, preferred_element_type=jnp.float32
    )

    def kernel(nb_ref, loc_ref, o_ref, a_ref, b_ref, out_ref, win_ref, cur_ref, inv_ref, mid_ref):
        odd = parity()
        win_ref[tiles : 2 * tiles] = o_ref[...]
        win_ref[pl.ds((1 - odd) * 2 * tiles, tiles)] = a_ref[...]
        win_ref[pl.ds(odd * 2 * tiles, tiles)] = b_ref[...]
        row = lax.broadcasted_iota(jnp.int32, (members, members), 0)
        col = lax.broadcasted_iota(jnp.int32, (members, members), 1)
        eye = (row == col).astype(jnp.float32)
        drives, scales = [], []
        for t in range(tiles):
            total = loc_ref[t, 0] * win_ref[nb_ref[t, 0]]
            for n in range(1, neigh):
                total = total + loc_ref[t, n] * win_ref[nb_ref[t, n]]
            curvature = (members - 1.0) * eye + jnp.concatenate(
                [total[0:half, 0:members], total[0:half, members:]], axis=0
            )
            drives.append(total[half : half + SUB, 0:members])
            square = jnp.sum(curvature * curvature, axis=0, keepdims=True)
            scale = jnp.sqrt(jnp.sum(square, axis=1, keepdims=True))
            scales.append(scale)
            cur_ref[t] = curvature / scale
        for step in range(NS_ITERS):
            for t in range(tiles):
                product = cur_ref[t] if step == 0 else dot(inv_ref[t], cur_ref[t])
                mid_ref[t] = 1.5 * eye - 0.5 * product
            for t in range(tiles):
                middle = mid_ref[t]
                if step < NS_ITERS - 1:
                    cur_ref[t] = dot(cur_ref[t], middle)
                inv_ref[t] = middle if step == 0 else dot(middle, inv_ref[t])
        for t in range(tiles):
            flipped = inv_ref[t].T
            half_step = dot(drives[t], flipped)
            mean_part = dot(half_step, flipped)[0:1] / scales[t]
            weights = jnp.sqrt((members - 1.0) / scales[t]) * flipped + mean_part
            rest = (1.0 - jnp.sum(weights, axis=1, keepdims=True)) * (1.0 / members)
            weights = weights + rest
            high = weights.astype(jnp.bfloat16).astype(jnp.float32)
            out_ref[t] = jnp.concatenate([high, weights - high], axis=1).astype(jnp.bfloat16)

    cube = pltpu.VMEM((tiles, members, members), jnp.float32)
    vmem = pl.BlockSpec(memory_space=pltpu.VMEM)
    smem = pl.BlockSpec(memory_space=pltpu.SMEM)
    return call(
        kernel,
        "transform",
        jax.ShapeDtypeStruct((tiles, members, lanes), jnp.bfloat16),
        2 * tiles * members**3 * 72,
        tiles * packed * lanes * 12,
        in_specs=[smem, smem, vmem, vmem, vmem],
        out_specs=vmem,
        scratch_shapes=[pltpu.VMEM((3 * tiles, packed, lanes), jnp.float32), cube, cube, cube],
    )(neighbours, localization, own, first, second)


def analyse(arrived, weights, mem_count, lat_count, lon_strip):
    sources, rows, lanes = arrived.shape
    members_dev = rows // lon_strip
    tiles, members, _ = weights.shape
    bands = lat_count // tiles
    group = lanes // SUB
    halves = lat_count // group
    per_member = group * halves * lon_strip
    chunks = members // SUB
    pitch = per_member + SUB

    def kernel(a_ref, w_ref, out_ref, product_ref, rows_ref, sem):
        @pl.loop(0, lon_strip)
        def _(x):
            at = pl.ds(pl.multiple_of(x * members_dev, members_dev), members_dev)
            for g in range(tiles):
                block = jnp.concatenate(
                    [
                        jnp.concatenate(
                            [a_ref[m * lat_count + g * bands + b, at, :] for m in range(mem_count)],
                            axis=0,
                        )
                        for b in range(bands)
                    ],
                    axis=1,
                )
                product = jnp.dot(
                    w_ref[g],
                    jnp.concatenate([block, block], axis=0),
                    preferred_element_type=jnp.float32,
                )
                for b in range(bands):
                    product_ref[x, g * bands + b] = product[:, b * lanes : (b + 1) * lanes]

        flat_ref = rows_ref.reshape(members * pitch, lanes)
        place = lax.broadcasted_iota(jnp.int32, (SUB, lanes), 1) // SUB

        def copy_out(j):
            at = pl.ds(j * SUB, SUB)
            return pltpu.make_async_copy(
                rows_ref.at[at, pl.ds(0, per_member)], out_ref.at[at], sem.at[j]
            )

        for j in range(chunks):
            at = pl.ds(j * SUB, SUB)
            for x in range(lon_strip):
                for half in range(halves):
                    held = [product_ref[x, half * group + b, at, :] for b in range(group)]
                    step = 1
                    while step < group:
                        odd = (place // step) % 2 == 1
                        held = [
                            jnp.where(odd, held[(r + step) % group], held[r]) for r in range(group)
                        ]
                        step *= 2
                    for c in range(group):
                        row = pltpu.roll(held[(-c) % group], (lanes - c * SUB) % lanes, 1)
                        first = j * SUB * pitch + (c * halves + half) * lon_strip + x
                        flat_ref[pl.ds(first, SUB, stride=pitch), :] = row
            copy_out(j).start()

        for j in range(chunks):
            copy_out(j).wait()

    vmem = pl.BlockSpec(memory_space=pltpu.VMEM)
    return call(
        kernel,
        "analyse",
        jax.ShapeDtypeStruct((members, per_member, lanes), jnp.float32),
        2 * tiles * members * 2 * members * bands * lanes * lon_strip,
        members * per_member * lanes * 6,
        in_specs=[vmem, vmem],
        out_specs=pl.BlockSpec(memory_space=pl.ANY),
        scratch_shapes=[
            pltpu.VMEM((lon_strip, lat_count, members, lanes), jnp.float32),
            pltpu.VMEM((members, pitch, lanes), jnp.float32),
            pltpu.SemaphoreType.DMA((chunks,)),
        ],
    )(arrived, weights)


def per_device(
    prior_member_stack,
    zonal_stability_ratio,
    meridional_stability_ratio,
    obs_perturb,
    innovation,
    inverse_error_variance,
    obs_count,
    neighbours,
    localization,
):
    members_dev, channels, row_count, lon_count = prior_member_stack.shape
    mem_count, lat_count = lax.axis_size("mem"), lax.axis_size("lat")
    devices = mem_count * lat_count
    lon_strip = lon_count // devices
    members = members_dev * mem_count

    first_rows, second_rows = edge_rows(
        prior_member_stack.reshape(members_dev * channels, row_count, lon_count),
        meridional_stability_ratio,
    )

    def swap(first, count, ring):
        pairs = [(i, (i + 1) % count) for i in range(first, count if ring else count - 1, 2)]
        return pairs + [(j, i) for i, j in pairs]

    first_rows = lax.ppermute(first_rows, "lat", swap(0, lat_count, False))
    second_rows = lax.ppermute(second_rows, "lat", swap(1, lat_count, False))

    sums = tile_sums(obs_perturb, innovation, inverse_error_variance, obs_count)
    first_rows, second_rows, sums = lax.optimization_barrier((first_rows, second_rows, sums))
    both = ("mem", "lat")
    first_sums = lax.ppermute(sums, both, swap(0, devices, True))
    second_sums = lax.ppermute(sums, both, swap(1, devices, True))

    sent = advect(
        prior_member_stack.reshape(members_dev, channels * row_count, lon_count),
        zonal_stability_ratio,
        meridional_stability_ratio,
        first_rows,
        second_rows,
        members_dev,
        channels,
    )
    sent = sent.reshape(devices, lon_strip * members_dev, channels * row_count)
    sent, first_sums, second_sums = lax.optimization_barrier((sent, first_sums, second_sums))
    arrived = lax.all_to_all(sent, both, split_axis=0, concat_axis=0, tiled=True)
    weights = transform(sums, first_sums, second_sums, neighbours, localization)
    rows = analyse(arrived, weights, mem_count, lat_count, lon_strip)
    halves = lat_count * row_count // LANES
    out = rows.reshape(members, channels, halves, lon_strip, LANES)
    out = jnp.transpose(out, (0, 1, 3, 2, 4))
    return out.reshape(members, channels, lon_strip, lat_count * row_count)


def solution(mesh):
    in_specs = (
        P("mem", None, "lat", None),
        P("lat", None),
        P("lat", None),
        P(("mem", "lat"), None, None),
        P(("mem", "lat"), None),
        P(("mem", "lat"), None),
        P(("mem", "lat")),
        P(("mem", "lat"), None),
        P(("mem", "lat"), None),
    )
    out_specs = P(None, None, ("mem", "lat"), None)
    return jax.shard_map(
        per_device, mesh=mesh, in_specs=in_specs, out_specs=out_specs, check_vma=False
    )
```

```python
import functools

import jax
import jax.numpy as jnp
from jax import lax
from jax.experimental import pallas as pl
from jax.experimental.pallas import tpu as pltpu
from jax.sharding import PartitionSpec as P

NS_ITERS = 5
LANES = 128
SUB = 8


def call(kernel, name, out_shape, flops, traffic, vmem=24, **kw):
    return pl.pallas_call(
        kernel,
        name=name,
        out_shape=out_shape,
        cost_estimate=pl.CostEstimate(flops=flops, bytes_accessed=traffic, transcendentals=0),
        compiler_params=pltpu.CompilerParams(vmem_limit_bytes=vmem << 20),
        **kw,
    )


def parity():
    return lax.rem(lax.axis_index("lat"), 2)


def edge_rows(prior, north):
    groups, sub, lon = prior.shape

    def kernel(q_ref, v_ref, first_ref, second_ref, north_ref, rows_ref, sem):
        odd = parity()
        copies = [
            pltpu.make_async_copy(q_ref.at[:, (sub - 1) * side, :], rows_ref.at[k], sem.at[k])
            for k, side in enumerate((1 - odd, odd))
        ]
        courant = pltpu.make_async_copy(v_ref, north_ref, sem.at[2])
        courant.start()
        for copy in copies:
            copy.start()
        courant.wait()
        v = jnp.broadcast_to(north_ref[sub - 1 : sub, :], (16, lon))
        high = v.astype(jnp.bfloat16).astype(jnp.float32)
        row = lax.broadcasted_iota(jnp.int32, (16, lon), 0)
        parts = jnp.where(row == 0, high, jnp.where(row == 1, v - high, 0.0)).astype(jnp.bfloat16)
        for k, ref in enumerate((first_ref, second_ref)):
            copies[k].wait()
            ref[0:groups, :] = rows_ref[k].astype(jnp.bfloat16)
            ref[groups : groups + 16, :] = parts

    out = jax.ShapeDtypeStruct((groups + 16, lon), jnp.bfloat16)
    vmem = pl.BlockSpec(memory_space=pltpu.VMEM)
    return call(
        kernel,
        "edge_rows",
        (out, out),
        groups * lon * 2,
        groups * lon * 12,
        vmem=52,
        in_specs=[pl.BlockSpec(memory_space=pl.ANY)] * 2,
        out_specs=(vmem, vmem),
        scratch_shapes=[
            pltpu.VMEM((sub, lon), jnp.float32),
            pltpu.VMEM((2, groups, lon), jnp.float32),
            pltpu.SemaphoreType.DMA((3,)),
        ],
    )(prior, north)


def advect(prior, zonal, north, first_rows, second_rows, members, channels):
    sub, lon = zonal.shape
    blocks = lon // LANES
    width = channels * sub
    edges = members * channels
    chunk = LANES * members
    pitch = members + SUB
    starts = (0, members // 4, members // 2)
    ends = starts[1:] + (members,)

    def kernel(
        q_hbm, u_ref, v_ref, ra_ref, rb_ref, out_ref,
        q_ref, coef_ref, halo_ref, adv_ref, rows_ref, sent_ref, in_sem, out_sem,
    ):
        def copy_in(group, b):
            some = pl.ds(starts[group], ends[group] - starts[group])
            return pltpu.make_async_copy(
                q_hbm.at[some, :, pl.ds(b * LANES, LANES)],
                q_ref.at[b, some, pl.ds(sub, width)],
                in_sem.at[group, b],
            )

        for group in range(len(starts)):
            for b in range(blocks):
                copy_in(group, b).start()

        odd = parity()
        u, v = u_ref[...], v_ref[...]
        row = lax.broadcasted_iota(jnp.int32, (sub, lon), 0)
        below = [ref[edges : edges + 16, :].astype(jnp.float32) for ref in (ra_ref, rb_ref)]
        below = jnp.where(odd == 1, below[0], below[1])
        below = jnp.broadcast_to(below[0:1] + below[1:2], (sub, lon))
        v_south = jnp.where(row == 0, below, pltpu.roll(v, 1, 0))
        u_west = pltpu.roll(u, 1, 1)
        vp, vn = jnp.maximum(v, 0.0), jnp.minimum(v, 0.0)
        vps, vns = jnp.maximum(v_south, 0.0), jnp.minimum(v_south, 0.0)
        coefs = (
            1.0 - jnp.maximum(u, 0.0) + jnp.minimum(u_west, 0.0) - vp + vns,
            -jnp.minimum(u, 0.0),
            jnp.maximum(u_west, 0.0),
            -vn,
            vps,
        )
        for k, coef in enumerate(coefs):
            for b in range(blocks):
                coef_ref[k, b] = coef[:, b * LANES : (b + 1) * LANES]
        lane = lax.broadcasted_iota(jnp.int32, (sub, LANES), 1)
        line = lax.broadcasted_iota(jnp.int32, (sub, LANES), 0)
        start = channels - lax.rem(lax.axis_index("lat"), channels)

        def stencil(member, slot):
            at = pl.ds(pl.multiple_of(member * channels, channels), channels)
            for k, ref in enumerate((ra_ref, rb_ref)):
                halo = ref[at, :].astype(jnp.float32)
                for b in range(blocks):
                    halo_ref[slot, k, b] = halo[:, b * LANES : (b + 1) * LANES]
            coef = [[coef_ref[k, b] for b in range(blocks)] for k in range(5)]
            for p in range(channels):
                c = lax.rem(start + p, channels)
                base = pl.multiple_of((c + 1) * sub, sub)
                q = [q_ref[b, member, pl.ds(base, sub), :] for b in range(blocks)]
                east = [pltpu.roll(x, LANES - 1, 1) for x in q]
                west = [pltpu.roll(x, 1, 1) for x in q]
                for b in range(blocks):
                    q_east = jnp.where(lane == LANES - 1, east[(b + 1) % blocks], east[b])
                    q_west = jnp.where(lane == 0, west[b - 1], west[b])
                    q_north = q_ref[b, member, pl.ds(base + 1, sub), :]
                    q_south = q_ref[b, member, pl.ds(base - 1, sub), :]
                    halo_south = halo_ref[slot, 1 - odd, b, pl.ds(c, 1), :]
                    halo_north = halo_ref[slot, odd, b, pl.ds(c, 1), :]
                    q_south = jnp.where(line == 0, halo_south, q_south)
                    q_north = jnp.where(line == sub - 1, halo_north, q_north)
                    adv_ref[member, b, p * sub : (p + 1) * sub, :] = (
                        q[b] * coef[0][b]
                        + q_east * coef[1][b]
                        + q_west * coef[2][b]
                        + q_north * coef[3][b]
                        + q_south * coef[4][b]
                    )

        @pl.loop(0, members // 4)
        def _(four):
            for group, first in enumerate(starts):

                @pl.when(four == first // 4)
                def _():
                    for b in range(blocks):
                        copy_in(group, b).wait()

            for k in range(4):
                stencil(four * 4 + k, k)

        copies = []
        for b in range(blocks):
            for member in range(members):
                at = pl.ds(member, LANES, stride=pitch)
                rows_ref[b % 2, at, :] = adv_ref[member, b].T
            for x in range(LANES):
                to = pl.ds(b * chunk + x * members, members)
                at = pl.ds(x * pitch, members)
                sent_ref[to, :] = rows_ref[b % 2, at, :].astype(jnp.bfloat16)
            at = pl.ds(b * chunk, chunk)
            copies.append(pltpu.make_async_copy(sent_ref.at[at], out_ref.at[at], out_sem.at[b]))
            copies[-1].start()
        for copy in copies:
            copy.wait()

    cells = members * channels * sub * lon
    vmem = pl.BlockSpec(memory_space=pltpu.VMEM)
    hbm = pl.BlockSpec(memory_space=pl.ANY)
    return call(
        kernel,
        "advect",
        jax.ShapeDtypeStruct((lon * members, width), jnp.bfloat16),
        cells * 10,
        cells * 6,
        vmem=52,
        in_specs=[hbm] + [vmem] * 4,
        out_specs=hbm,
        scratch_shapes=[
            pltpu.VMEM((blocks, members, width + 2 * sub, LANES), jnp.float32),
            pltpu.VMEM((5, blocks, sub, LANES), jnp.float32),
            pltpu.VMEM((4, 2, blocks, channels, LANES), jnp.float32),
            pltpu.VMEM((members, blocks, width, LANES), jnp.float32),
            pltpu.VMEM((2, (LANES + 1) * pitch, width), jnp.float32),
            pltpu.VMEM((lon * members, width), jnp.bfloat16),
            pltpu.SemaphoreType.DMA((len(starts), blocks)),
            pltpu.SemaphoreType.DMA((blocks,)),
        ],
    )(prior, zonal, north, first_rows, second_rows)


def tile_sums(perturb, innovation, inverse_error_variance, obs_count):
    tiles, members, cap = perturb.shape
    half = members // 2
    parts = 4
    per_part = tiles // parts

    def kernel(count_ref, p_ref, inn_ref, iev_ref, out_ref, held_ref, sem):
        copies = [
            pltpu.make_async_copy(
                p_ref.at[pl.ds(i * per_part, per_part)],
                held_ref.at[pl.ds(i * per_part, per_part)],
                sem.at[i],
            )
            for i in range(parts)
        ]
        for copy in copies:
            copy.start()
        slot = lax.broadcasted_iota(jnp.int32, (1, cap), 1)
        for tile in range(tiles):
            if tile % per_part == 0:
                copies[tile // per_part].wait()
            valid = slot < count_ref[tile]
            iev = iev_ref[tile : tile + 1, :]
            weight = jnp.where(valid, iev, 0.0)
            drive = jnp.where(valid, iev * inn_ref[tile : tile + 1, :], 0.0)
            weight = jnp.broadcast_to(weight, (16, cap)).astype(jnp.bfloat16)
            drive = jnp.broadcast_to(drive, (16, cap)).astype(jnp.bfloat16)
            p = held_ref[tile]
            left = jnp.concatenate(
                [p[i * 16 : (i + 1) * 16] * weight for i in range(members // 16)] + [drive], axis=0
            )
            sums = lax.dot_general(
                left, p, (((1,), (1,)), ((), ())), preferred_element_type=jnp.float32
            )
            out_ref[tile, 0:half, :] = jnp.concatenate([sums[0:half], sums[half:members]], axis=1)
            last = sums[members : members + SUB]
            out_ref[tile, half : half + SUB, :] = jnp.concatenate([last, last], axis=1)

    vmem = pl.BlockSpec(memory_space=pltpu.VMEM)
    return call(
        kernel,
        "tile_sums",
        jax.ShapeDtypeStruct((tiles, half + SUB, 2 * members), jnp.float32),
        2 * tiles * members * (members + 16) * cap,
        tiles * members * cap * 2,
        vmem=50,
        in_specs=[
            pl.BlockSpec(memory_space=pltpu.SMEM),
            pl.BlockSpec(memory_space=pl.ANY),
            vmem,
            vmem,
        ],
        out_specs=vmem,
        scratch_shapes=[
            pltpu.VMEM((tiles, members, cap), jnp.bfloat16),
            pltpu.SemaphoreType.DMA((parts,)),
        ],
    )(obs_count, perturb, innovation, inverse_error_variance)


def transform(own, first, second, neighbours, localization):
    tiles, packed, lanes = own.shape
    members = lanes // 2
    half = members // 2
    neigh = neighbours.shape[1]
    dot = functools.partial(
        jnp.dot, precision=lax.Precision.HIGHEST, preferred_element_type=jnp.float32
    )

    def kernel(nb_ref, loc_ref, o_ref, a_ref, b_ref, out_ref, win_ref, cur_ref, inv_ref, mid_ref):
        odd = parity()
        win_ref[tiles : 2 * tiles] = o_ref[...]
        win_ref[pl.ds((1 - odd) * 2 * tiles, tiles)] = a_ref[...]
        win_ref[pl.ds(odd * 2 * tiles, tiles)] = b_ref[...]
        row = lax.broadcasted_iota(jnp.int32, (members, members), 0)
        col = lax.broadcasted_iota(jnp.int32, (members, members), 1)
        eye = (row == col).astype(jnp.float32)
        drives, scales = [], []
        for t in range(tiles):
            total = loc_ref[t, 0] * win_ref[nb_ref[t, 0]]
            for n in range(1, neigh):
                total = total + loc_ref[t, n] * win_ref[nb_ref[t, n]]
            curvature = (members - 1.0) * eye + jnp.concatenate(
                [total[0:half, 0:members], total[0:half, members:]], axis=0
            )
            drives.append(total[half : half + SUB, 0:members])
            square = jnp.sum(curvature * curvature, axis=0, keepdims=True)
            scale = jnp.sqrt(jnp.sum(square, axis=1, keepdims=True))
            scales.append(scale)
            cur_ref[t] = curvature / scale
        for step in range(NS_ITERS):
            for t in range(tiles):
                product = cur_ref[t] if step == 0 else dot(inv_ref[t], cur_ref[t])
                mid_ref[t] = 1.5 * eye - 0.5 * product
            for t in range(tiles):
                middle = mid_ref[t]
                if step < NS_ITERS - 1:
                    cur_ref[t] = dot(cur_ref[t], middle)
                inv_ref[t] = middle if step == 0 else dot(middle, inv_ref[t])
        for t in range(tiles):
            flipped = inv_ref[t].T
            half_step = dot(drives[t], flipped)
            mean_part = dot(half_step, flipped)[0:1] / scales[t]
            weights = jnp.sqrt((members - 1.0) / scales[t]) * flipped + mean_part
            rest = (1.0 - jnp.sum(weights, axis=1, keepdims=True)) * (1.0 / members)
            weights = weights + rest
            high = weights.astype(jnp.bfloat16).astype(jnp.float32)
            out_ref[t] = jnp.concatenate([high, weights - high], axis=1).astype(jnp.bfloat16)

    cube = pltpu.VMEM((tiles, members, members), jnp.float32)
    vmem = pl.BlockSpec(memory_space=pltpu.VMEM)
    smem = pl.BlockSpec(memory_space=pltpu.SMEM)
    return call(
        kernel,
        "transform",
        jax.ShapeDtypeStruct((tiles, members, lanes), jnp.bfloat16),
        2 * tiles * members**3 * 72,
        tiles * packed * lanes * 12,
        in_specs=[smem, smem, vmem, vmem, vmem],
        out_specs=vmem,
        scratch_shapes=[pltpu.VMEM((3 * tiles, packed, lanes), jnp.float32), cube, cube, cube],
    )(neighbours, localization, own, first, second)


def analyse(arrived, weights, mem_count, lat_count, lon_strip):
    sources, rows, lanes = arrived.shape
    members_dev = rows // lon_strip
    tiles, members, _ = weights.shape
    bands = lat_count // tiles
    group = lanes // SUB
    halves = lat_count // group
    per_member = group * halves * lon_strip
    chunks = members // SUB
    pitch = per_member + SUB

    def kernel(a_ref, w_ref, out_ref, product_ref, rows_ref, sem):
        for x in range(lon_strip):
            at = pl.ds(x * members_dev, members_dev)
            for g in range(tiles):
                block = jnp.concatenate(
                    [
                        jnp.concatenate(
                            [a_ref[m * lat_count + g * bands + b, at, :] for m in range(mem_count)],
                            axis=0,
                        )
                        for b in range(bands)
                    ],
                    axis=1,
                )
                product = jnp.dot(
                    w_ref[g],
                    jnp.concatenate([block, block], axis=0),
                    preferred_element_type=jnp.float32,
                )
                for b in range(bands):
                    product_ref[x, g * bands + b] = product[:, b * lanes : (b + 1) * lanes]

        flat_ref = rows_ref.reshape((members + 1) * pitch, lanes)
        place = lax.broadcasted_iota(jnp.int32, (SUB, lanes), 1) // SUB

        def copy_out(j):
            at = pl.ds(j * SUB, SUB)
            return pltpu.make_async_copy(
                rows_ref.at[at, pl.ds(0, per_member)], out_ref.at[at], sem.at[j]
            )

        for j in range(chunks):
            at = pl.ds(j * SUB, SUB)
            for x in range(lon_strip):
                for half in range(halves):
                    held = [product_ref[x, half * group + b, at, :] for b in range(group)]
                    step = 1
                    while step < group:
                        odd = (place // step) % 2 == 1
                        held = [
                            jnp.where(odd, held[(r + step) % group], held[r]) for r in range(group)
                        ]
                        step *= 2
                    for c in range(group):
                        row = pltpu.roll(held[(-c) % group], (lanes - c * SUB) % lanes, 1)
                        first = j * SUB * pitch + (c * halves + half) * lon_strip + x
                        flat_ref[pl.ds(first, SUB, stride=pitch), :] = row
            copy_out(j).start()

        for j in range(chunks):
            copy_out(j).wait()

    vmem = pl.BlockSpec(memory_space=pltpu.VMEM)
    return call(
        kernel,
        "analyse",
        jax.ShapeDtypeStruct((members, per_member, lanes), jnp.float32),
        2 * tiles * members * 2 * members * bands * lanes * lon_strip,
        members * per_member * lanes * 6,
        in_specs=[vmem, vmem],
        out_specs=pl.BlockSpec(memory_space=pl.ANY),
        scratch_shapes=[
            pltpu.VMEM((lon_strip, lat_count, members, lanes), jnp.float32),
            pltpu.VMEM((members + 1, pitch, lanes), jnp.float32),
            pltpu.SemaphoreType.DMA((chunks,)),
        ],
    )(arrived, weights)


def per_device(
    prior_member_stack,
    zonal_stability_ratio,
    meridional_stability_ratio,
    obs_perturb,
    innovation,
    inverse_error_variance,
    obs_count,
    neighbours,
    localization,
):
    members_dev, channels, row_count, lon_count = prior_member_stack.shape
    mem_count, lat_count = lax.axis_size("mem"), lax.axis_size("lat")
    devices = mem_count * lat_count
    lon_strip = lon_count // devices
    members = members_dev * mem_count

    first_rows, second_rows = edge_rows(
        prior_member_stack.reshape(members_dev * channels, row_count, lon_count),
        meridional_stability_ratio,
    )

    def swap(first, count, ring):
        pairs = [(i, (i + 1) % count) for i in range(first, count if ring else count - 1, 2)]
        return pairs + [(j, i) for i, j in pairs]

    first_rows = lax.ppermute(first_rows, "lat", swap(0, lat_count, False))
    second_rows = lax.ppermute(second_rows, "lat", swap(1, lat_count, False))

    sums = tile_sums(obs_perturb, innovation, inverse_error_variance, obs_count)
    first_rows, second_rows, sums = lax.optimization_barrier((first_rows, second_rows, sums))
    both = ("mem", "lat")
    first_sums = lax.ppermute(sums, both, swap(0, devices, True))
    second_sums = lax.ppermute(sums, both, swap(1, devices, True))

    sent = advect(
        prior_member_stack.reshape(members_dev, channels * row_count, lon_count),
        zonal_stability_ratio,
        meridional_stability_ratio,
        first_rows,
        second_rows,
        members_dev,
        channels,
    )
    sent = sent.reshape(devices, lon_strip * members_dev, channels * row_count)
    sent, first_sums, second_sums = lax.optimization_barrier((sent, first_sums, second_sums))
    arrived = lax.all_to_all(sent, both, split_axis=0, concat_axis=0, tiled=True)
    weights = transform(sums, first_sums, second_sums, neighbours, localization)
    rows = analyse(arrived, weights, mem_count, lat_count, lon_strip)
    halves = lat_count * row_count // LANES
    out = rows.reshape(members, channels, halves, lon_strip, LANES)
    out = jnp.transpose(out, (0, 1, 3, 2, 4))
    return out.reshape(members, channels, lon_strip, lat_count * row_count)


def solution(mesh):
    in_specs = (
        P("mem", None, "lat", None),
        P("lat", None),
        P("lat", None),
        P(("mem", "lat"), None, None),
        P(("mem", "lat"), None),
        P(("mem", "lat"), None),
        P(("mem", "lat")),
        P(("mem", "lat"), None),
        P(("mem", "lat"), None),
    )
    out_specs = P(None, None, ("mem", "lat"), None)
    return jax.shard_map(
        per_device, mesh=mesh, in_specs=in_specs, out_specs=out_specs, check_vma=False
    )
```

```python
import functools

import jax
import jax.numpy as jnp
from jax import lax
from jax.experimental import pallas as pl
from jax.experimental.pallas import tpu as pltpu
from jax.sharding import PartitionSpec as P

NS_ITERS = 5
LANES = 128
SUB = 8


def call(kernel, name, out_shape, flops, traffic, vmem=24, **kw):
    return pl.pallas_call(
        kernel,
        name=name,
        out_shape=out_shape,
        cost_estimate=pl.CostEstimate(flops=flops, bytes_accessed=traffic, transcendentals=0),
        compiler_params=pltpu.CompilerParams(vmem_limit_bytes=vmem << 20),
        **kw,
    )


def parity():
    return lax.rem(lax.axis_index("lat"), 2)


def edge_rows(prior, north):
    groups, sub, lon = prior.shape

    def kernel(q_ref, v_ref, first_ref, second_ref, north_ref, rows_ref, sent_ref, sem, out_sem):
        odd = parity()
        copies = [
            pltpu.make_async_copy(q_ref.at[:, (sub - 1) * side, :], rows_ref.at[k], sem.at[k])
            for k, side in enumerate((1 - odd, odd))
        ]
        courant = pltpu.make_async_copy(v_ref, north_ref, sem.at[2])
        courant.start()
        for copy in copies:
            copy.start()
        courant.wait()
        v = jnp.broadcast_to(north_ref[sub - 1 : sub, :], (16, lon))
        high = v.astype(jnp.bfloat16).astype(jnp.float32)
        row = lax.broadcasted_iota(jnp.int32, (16, lon), 0)
        parts = jnp.where(row == 0, high, jnp.where(row == 1, v - high, 0.0)).astype(jnp.bfloat16)
        leaving = []
        for k, ref in enumerate((first_ref, second_ref)):
            copies[k].wait()
            sent_ref[k, 0:groups, :] = rows_ref[k].astype(jnp.bfloat16)
            sent_ref[k, groups : groups + 16, :] = parts
            leaving.append(pltpu.make_async_copy(sent_ref.at[k], ref, out_sem.at[k]))
            leaving[k].start()
        for copy in leaving:
            copy.wait()

    out = jax.ShapeDtypeStruct((groups + 16, lon), jnp.bfloat16)
    return call(
        kernel,
        "edge_rows",
        [out, out],
        groups * lon * 2,
        groups * lon * 12,
        vmem=54,
        in_specs=[pl.BlockSpec(memory_space=pl.ANY)] * 2,
        out_specs=[pl.BlockSpec(memory_space=pl.ANY)] * 2,
        scratch_shapes=[
            pltpu.VMEM((sub, lon), jnp.float32),
            pltpu.VMEM((2, groups, lon), jnp.float32),
            pltpu.VMEM((2, groups + 16, lon), jnp.bfloat16),
            pltpu.SemaphoreType.DMA((3,)),
            pltpu.SemaphoreType.DMA((2,)),
        ],
    )(prior, north)


def advect(prior, zonal, north, first_rows, second_rows, members, channels):
    sub, lon = zonal.shape
    blocks = lon // LANES
    width = channels * sub
    edges = members * channels
    chunk = LANES * members
    pitch = members + SUB
    starts = (0, members // 4, members // 2)
    ends = starts[1:] + (members,)

    def kernel(
        q_hbm, u_ref, v_ref, ra_ref, rb_ref, out_ref,
        q_ref, coef_ref, halo_ref, adv_ref, rows_ref, sent_ref, in_sem, out_sem,
    ):
        def copy_in(group, b):
            some = pl.ds(starts[group], ends[group] - starts[group])
            return pltpu.make_async_copy(
                q_hbm.at[some, :, pl.ds(b * LANES, LANES)],
                q_ref.at[b, some, pl.ds(sub, width)],
                in_sem.at[group, b],
            )

        for group in range(len(starts)):
            for b in range(blocks):
                copy_in(group, b).start()

        odd = parity()
        u, v = u_ref[...], v_ref[...]
        row = lax.broadcasted_iota(jnp.int32, (sub, lon), 0)
        below = [ref[edges : edges + 16, :].astype(jnp.float32) for ref in (ra_ref, rb_ref)]
        below = jnp.where(odd == 1, below[0], below[1])
        below = jnp.broadcast_to(below[0:1] + below[1:2], (sub, lon))
        v_south = jnp.where(row == 0, below, pltpu.roll(v, 1, 0))
        u_west = pltpu.roll(u, 1, 1)
        vp, vn = jnp.maximum(v, 0.0), jnp.minimum(v, 0.0)
        vps, vns = jnp.maximum(v_south, 0.0), jnp.minimum(v_south, 0.0)
        coefs = (
            1.0 - jnp.maximum(u, 0.0) + jnp.minimum(u_west, 0.0) - vp + vns,
            -jnp.minimum(u, 0.0),
            jnp.maximum(u_west, 0.0),
            -vn,
            vps,
        )
        for k, coef in enumerate(coefs):
            for b in range(blocks):
                coef_ref[k, b] = coef[:, b * LANES : (b + 1) * LANES]
        lane = lax.broadcasted_iota(jnp.int32, (sub, LANES), 1)
        line = lax.broadcasted_iota(jnp.int32, (sub, LANES), 0)
        start = channels - lax.rem(lax.axis_index("lat"), channels)

        def stencil(member, slot):
            at = pl.ds(pl.multiple_of(member * channels, channels), channels)
            for k, ref in enumerate((ra_ref, rb_ref)):
                halo = ref[at, :].astype(jnp.float32)
                for b in range(blocks):
                    halo_ref[slot, k, b] = halo[:, b * LANES : (b + 1) * LANES]
            coef = [[coef_ref[k, b] for b in range(blocks)] for k in range(5)]
            for p in range(channels):
                c = lax.rem(start + p, channels)
                base = pl.multiple_of((c + 1) * sub, sub)
                q = [q_ref[b, member, pl.ds(base, sub), :] for b in range(blocks)]
                east = [pltpu.roll(x, LANES - 1, 1) for x in q]
                west = [pltpu.roll(x, 1, 1) for x in q]
                for b in range(blocks):
                    q_east = jnp.where(lane == LANES - 1, east[(b + 1) % blocks], east[b])
                    q_west = jnp.where(lane == 0, west[b - 1], west[b])
                    q_north = q_ref[b, member, pl.ds(base + 1, sub), :]
                    q_south = q_ref[b, member, pl.ds(base - 1, sub), :]
                    halo_south = halo_ref[slot, 1 - odd, b, pl.ds(c, 1), :]
                    halo_north = halo_ref[slot, odd, b, pl.ds(c, 1), :]
                    q_south = jnp.where(line == 0, halo_south, q_south)
                    q_north = jnp.where(line == sub - 1, halo_north, q_north)
                    adv_ref[member, b, p * sub : (p + 1) * sub, :] = (
                        q[b] * coef[0][b]
                        + q_east * coef[1][b]
                        + q_west * coef[2][b]
                        + q_north * coef[3][b]
                        + q_south * coef[4][b]
                    )

        @pl.loop(0, members // 4)
        def _(four):
            for group, first in enumerate(starts):

                @pl.when(four == first // 4)
                def _():
                    for b in range(blocks):
                        copy_in(group, b).wait()

            for k in range(4):
                stencil(four * 4 + k, k)

        copies = []
        for b in range(blocks):
            for member in range(members):
                at = pl.ds(member, LANES, stride=pitch)
                rows_ref[b % 2, at, :] = adv_ref[member, b].T
            for x in range(LANES):
                to = pl.ds(b * chunk + x * members, members)
                at = pl.ds(x * pitch, members)
                sent_ref[to, :] = rows_ref[b % 2, at, :].astype(jnp.bfloat16)
            at = pl.ds(b * chunk, chunk)
            copies.append(pltpu.make_async_copy(sent_ref.at[at], out_ref.at[at], out_sem.at[b]))
            copies[-1].start()
        for copy in copies:
            copy.wait()

    cells = members * channels * sub * lon
    vmem = pl.BlockSpec(memory_space=pltpu.VMEM)
    hbm = pl.BlockSpec(memory_space=pl.ANY)
    return call(
        kernel,
        "advect",
        jax.ShapeDtypeStruct((lon * members, width), jnp.bfloat16),
        cells * 10,
        cells * 6,
        vmem=52,
        in_specs=[hbm] + [vmem] * 4,
        out_specs=hbm,
        scratch_shapes=[
            pltpu.VMEM((blocks, members, width + 2 * sub, LANES), jnp.float32),
            pltpu.VMEM((5, blocks, sub, LANES), jnp.float32),
            pltpu.VMEM((4, 2, blocks, channels, LANES), jnp.float32),
            pltpu.VMEM((members, blocks, width, LANES), jnp.float32),
            pltpu.VMEM((2, (LANES + 1) * pitch, width), jnp.float32),
            pltpu.VMEM((lon * members, width), jnp.bfloat16),
            pltpu.SemaphoreType.DMA((len(starts), blocks)),
            pltpu.SemaphoreType.DMA((blocks,)),
        ],
    )(prior, zonal, north, first_rows, second_rows)


def tile_sums(perturb, innovation, inverse_error_variance, obs_count):
    tiles, members, cap = perturb.shape
    half = members // 2
    parts = 4
    per_part = tiles // parts

    def kernel(count_ref, p_ref, inn_ref, iev_ref, out_ref, held_ref, sem):
        copies = [
            pltpu.make_async_copy(
                p_ref.at[pl.ds(i * per_part, per_part)],
                held_ref.at[pl.ds(i * per_part, per_part)],
                sem.at[i],
            )
            for i in range(parts)
        ]
        for copy in copies:
            copy.start()
        slot = lax.broadcasted_iota(jnp.int32, (1, cap), 1)
        for tile in range(tiles):
            if tile % per_part == 0:
                copies[tile // per_part].wait()
            valid = slot < count_ref[tile]
            iev = iev_ref[tile : tile + 1, :]
            weight = jnp.where(valid, iev, 0.0)
            drive = jnp.where(valid, iev * inn_ref[tile : tile + 1, :], 0.0)
            weight = jnp.broadcast_to(weight, (16, cap)).astype(jnp.bfloat16)
            drive = jnp.broadcast_to(drive, (16, cap)).astype(jnp.bfloat16)
            p = held_ref[tile]
            left = jnp.concatenate(
                [p[i * 16 : (i + 1) * 16] * weight for i in range(members // 16)] + [drive], axis=0
            )
            sums = lax.dot_general(
                left, p, (((1,), (1,)), ((), ())), preferred_element_type=jnp.float32
            )
            out_ref[tile, 0:half, :] = jnp.concatenate([sums[0:half], sums[half:members]], axis=1)
            last = sums[members : members + SUB]
            out_ref[tile, half : half + SUB, :] = jnp.concatenate([last, last], axis=1)

    vmem = pl.BlockSpec(memory_space=pltpu.VMEM)
    return call(
        kernel,
        "tile_sums",
        jax.ShapeDtypeStruct((tiles, half + SUB, 2 * members), jnp.float32),
        2 * tiles * members * (members + 16) * cap,
        tiles * members * cap * 2,
        vmem=50,
        in_specs=[
            pl.BlockSpec(memory_space=pltpu.SMEM),
            pl.BlockSpec(memory_space=pl.ANY),
            vmem,
            vmem,
        ],
        out_specs=vmem,
        scratch_shapes=[
            pltpu.VMEM((tiles, members, cap), jnp.bfloat16),
            pltpu.SemaphoreType.DMA((parts,)),
        ],
    )(obs_count, perturb, innovation, inverse_error_variance)


def transform(own, first, second, neighbours, localization):
    tiles, packed, lanes = own.shape
    members = lanes // 2
    half = members // 2
    neigh = neighbours.shape[1]
    dot = functools.partial(
        jnp.dot, precision=lax.Precision.HIGHEST, preferred_element_type=jnp.float32
    )

    def kernel(nb_ref, loc_ref, o_ref, a_ref, b_ref, out_ref, win_ref, cur_ref, inv_ref, mid_ref):
        odd = parity()
        win_ref[tiles : 2 * tiles] = o_ref[...]
        win_ref[pl.ds((1 - odd) * 2 * tiles, tiles)] = a_ref[...]
        win_ref[pl.ds(odd * 2 * tiles, tiles)] = b_ref[...]
        row = lax.broadcasted_iota(jnp.int32, (members, members), 0)
        col = lax.broadcasted_iota(jnp.int32, (members, members), 1)
        eye = (row == col).astype(jnp.float32)
        drives, scales = [], []
        for t in range(tiles):
            total = loc_ref[t, 0] * win_ref[nb_ref[t, 0]]
            for n in range(1, neigh):
                total = total + loc_ref[t, n] * win_ref[nb_ref[t, n]]
            curvature = (members - 1.0) * eye + jnp.concatenate(
                [total[0:half, 0:members], total[0:half, members:]], axis=0
            )
            drives.append(total[half : half + SUB, 0:members])
            square = jnp.sum(curvature * curvature, axis=0, keepdims=True)
            scale = jnp.sqrt(jnp.sum(square, axis=1, keepdims=True))
            scales.append(scale)
            cur_ref[t] = curvature / scale
        for step in range(NS_ITERS):
            for t in range(tiles):
                product = cur_ref[t] if step == 0 else dot(inv_ref[t], cur_ref[t])
                mid_ref[t] = 1.5 * eye - 0.5 * product
            for t in range(tiles):
                middle = mid_ref[t]
                if step < NS_ITERS - 1:
                    cur_ref[t] = dot(cur_ref[t], middle)
                inv_ref[t] = middle if step == 0 else dot(middle, inv_ref[t])
        for t in range(tiles):
            flipped = inv_ref[t].T
            half_step = dot(drives[t], flipped)
            mean_part = dot(half_step, flipped)[0:1] / scales[t]
            weights = jnp.sqrt((members - 1.0) / scales[t]) * flipped + mean_part
            rest = (1.0 - jnp.sum(weights, axis=1, keepdims=True)) * (1.0 / members)
            weights = weights + rest
            high = weights.astype(jnp.bfloat16).astype(jnp.float32)
            out_ref[t] = jnp.concatenate([high, weights - high], axis=1).astype(jnp.bfloat16)

    cube = pltpu.VMEM((tiles, members, members), jnp.float32)
    vmem = pl.BlockSpec(memory_space=pltpu.VMEM)
    smem = pl.BlockSpec(memory_space=pltpu.SMEM)
    return call(
        kernel,
        "transform",
        jax.ShapeDtypeStruct((tiles, members, lanes), jnp.bfloat16),
        2 * tiles * members**3 * 72,
        tiles * packed * lanes * 12,
        in_specs=[smem, smem, vmem, vmem, vmem],
        out_specs=vmem,
        scratch_shapes=[pltpu.VMEM((3 * tiles, packed, lanes), jnp.float32), cube, cube, cube],
    )(neighbours, localization, own, first, second)


def analyse(arrived, weights, mem_count, lat_count, lon_strip):
    sources, rows, lanes = arrived.shape
    members_dev = rows // lon_strip
    tiles, members, _ = weights.shape
    bands = lat_count // tiles
    group = lanes // SUB
    halves = lat_count // group
    per_member = group * halves * lon_strip
    chunks = members // SUB
    pitch = per_member + SUB

    def kernel(a_ref, w_ref, out_ref, product_ref, rows_ref, sem):
        for x in range(lon_strip):
            at = pl.ds(x * members_dev, members_dev)
            for g in range(tiles):
                block = jnp.concatenate(
                    [
                        jnp.concatenate(
                            [a_ref[m * lat_count + g * bands + b, at, :] for m in range(mem_count)],
                            axis=0,
                        )
                        for b in range(bands)
                    ],
                    axis=1,
                )
                product = jnp.dot(
                    w_ref[g],
                    jnp.concatenate([block, block], axis=0),
                    preferred_element_type=jnp.float32,
                )
                for b in range(bands):
                    product_ref[x, g * bands + b] = product[:, b * lanes : (b + 1) * lanes]

        flat_ref = rows_ref.reshape((members + 1) * pitch, lanes)
        place = lax.broadcasted_iota(jnp.int32, (SUB, lanes), 1) // SUB

        def copy_out(j):
            at = pl.ds(j * SUB, SUB)
            return pltpu.make_async_copy(
                rows_ref.at[at, pl.ds(0, per_member)], out_ref.at[at], sem.at[j]
            )

        for j in range(chunks):
            at = pl.ds(j * SUB, SUB)
            for x in range(lon_strip):
                for half in range(halves):
                    held = [product_ref[x, half * group + b, at, :] for b in range(group)]
                    step = 1
                    while step < group:
                        odd = (place // step) % 2 == 1
                        held = [
                            jnp.where(odd, held[(r + step) % group], held[r]) for r in range(group)
                        ]
                        step *= 2
                    for c in range(group):
                        row = pltpu.roll(held[(-c) % group], (lanes - c * SUB) % lanes, 1)
                        first = j * SUB * pitch + (c * halves + half) * lon_strip + x
                        flat_ref[pl.ds(first, SUB, stride=pitch), :] = row
            copy_out(j).start()

        for j in range(chunks):
            copy_out(j).wait()

    vmem = pl.BlockSpec(memory_space=pltpu.VMEM)
    return call(
        kernel,
        "analyse",
        jax.ShapeDtypeStruct((members, per_member, lanes), jnp.float32),
        2 * tiles * members * 2 * members * bands * lanes * lon_strip,
        members * per_member * lanes * 6,
        in_specs=[vmem, vmem],
        out_specs=pl.BlockSpec(memory_space=pl.ANY),
        scratch_shapes=[
            pltpu.VMEM((lon_strip, lat_count, members, lanes), jnp.float32),
            pltpu.VMEM((members + 1, pitch, lanes), jnp.float32),
            pltpu.SemaphoreType.DMA((chunks,)),
        ],
    )(arrived, weights)


def per_device(
    prior_member_stack,
    zonal_stability_ratio,
    meridional_stability_ratio,
    obs_perturb,
    innovation,
    inverse_error_variance,
    obs_count,
    neighbours,
    localization,
):
    members_dev, channels, row_count, lon_count = prior_member_stack.shape
    mem_count, lat_count = lax.axis_size("mem"), lax.axis_size("lat")
    devices = mem_count * lat_count
    lon_strip = lon_count // devices
    members = members_dev * mem_count

    first_rows, second_rows = edge_rows(
        prior_member_stack.reshape(members_dev * channels, row_count, lon_count),
        meridional_stability_ratio,
    )

    def swap(first, count, ring):
        pairs = [(i, (i + 1) % count) for i in range(first, count if ring else count - 1, 2)]
        return pairs + [(j, i) for i, j in pairs]

    first_rows = lax.ppermute(first_rows, "lat", swap(0, lat_count, False))
    second_rows = lax.ppermute(second_rows, "lat", swap(1, lat_count, False))

    sums = tile_sums(obs_perturb, innovation, inverse_error_variance, obs_count)
    first_rows, second_rows, sums = lax.optimization_barrier((first_rows, second_rows, sums))
    both = ("mem", "lat")
    first_sums = lax.ppermute(sums, both, swap(0, devices, True))
    second_sums = lax.ppermute(sums, both, swap(1, devices, True))

    sent = advect(
        prior_member_stack.reshape(members_dev, channels * row_count, lon_count),
        zonal_stability_ratio,
        meridional_stability_ratio,
        first_rows,
        second_rows,
        members_dev,
        channels,
    )
    sent = sent.reshape(devices, lon_strip * members_dev, channels * row_count)
    sent, first_sums, second_sums = lax.optimization_barrier((sent, first_sums, second_sums))
    arrived = lax.all_to_all(sent, both, split_axis=0, concat_axis=0, tiled=True)
    weights = transform(sums, first_sums, second_sums, neighbours, localization)
    rows = analyse(arrived, weights, mem_count, lat_count, lon_strip)
    halves = lat_count * row_count // LANES
    out = rows.reshape(members, channels, halves, lon_strip, LANES)
    out = jnp.transpose(out, (0, 1, 3, 2, 4))
    return out.reshape(members, channels, lon_strip, lat_count * row_count)


def solution(mesh):
    in_specs = (
        P("mem", None, "lat", None),
        P("lat", None),
        P("lat", None),
        P(("mem", "lat"), None, None),
        P(("mem", "lat"), None),
        P(("mem", "lat"), None),
        P(("mem", "lat")),
        P(("mem", "lat"), None),
        P(("mem", "lat"), None),
    )
    out_specs = P(None, None, ("mem", "lat"), None)
    return jax.shard_map(
        per_device, mesh=mesh, in_specs=in_specs, out_specs=out_specs, check_vma=False
    )
```
